32 devices in a mesh: groups: 2 (over x), cols: 8 (over z, y), comp: 2 (over core).
Axes of the slice: x: 2, y: 2, z: 4, core: 2. Of those that a mesh axis runs over, the one named last changes fastest.
Arguments:
- zonal_current: float32 [64, 256, 128], P(None, ('groups', 'cols', 'comp')), parts along dimension 1, may hold values from -3 to 3
- meridional_current: float32 [64, 256, 128], P(None, ('groups', 'cols', 'comp')), parts along dimension 1, may hold values from -3 to 3
- thermal_anomaly: float32 [64, 256, 128], P(None, ('groups', 'cols', 'comp')), parts along dimension 1, may hold values from -5 to 5
- saltiness_anomaly: float32 [64, 256, 128], P(None, ('groups', 'cols', 'comp')), parts along dimension 1, may hold values from -5 to 5
- species_amounts: float32 [16, 64, 32768], P(None, None, ('groups', 'cols', 'comp')), parts along dimension 2, may hold values from -5 to 5
- wet_layer_number: int32 [256, 128], P(('groups', 'cols', 'comp')), parts along dimension 0, may hold values from 0 to 64
- profile_block_order: int32 [256, 128], P(('groups', 'cols', 'comp')), parts along dimension 0, may hold values from 0 to 16383, as said below
- species_coupling: float32 [16, 16], replicated, may hold values from -1.5 to 1.5
- settling_fraction: float32 [16], replicated, may hold values from 0.05 to 0.5
Outputs:
- out_u: float32 [64, 256, 128], P(None, ('groups', 'cols', 'comp')), parts along dimension 1
- out_v: float32 [64, 256, 128], P(None, ('groups', 'cols', 'comp')), parts along dimension 1
- out_temperature: float32 [64, 256, 128], P(None, ('groups', 'cols', 'comp')), parts along dimension 1
- out_salinity: float32 [64, 256, 128], P(None, ('groups', 'cols', 'comp')), parts along dimension 1
- out_tracers: float32 [16, 64, 32768], P(None, None, ('groups', 'cols', 'comp')), parts along dimension 2
The draws below stay inside these ranges and needn't reach their ends.
There are 2 independent parts, one for each index of `groups`. The reference program is written for one: setup_inputs(seed, part) draws one part's arguments, and reference() takes and returns one part's arrays. A program takes and returns all parts, laid end to end along the dimension named above; an argument that names none is the same for every part. Nothing has to cross between parts.
Inputs may be any that keep to these rules, and one draw needn't show every extreme that they name: profile_block_order holds each of 0 to 16383 once; the 1024 columns of tile t (longitudes t * 8 on) give exactly 64 columns to each patch d (positions d * 1024 to (d + 1) * 1024 - 1), placed at d * 1024 + t * 64 + r for r below 64.
All inputs are finite; a program needn't handle non-finite values.
Results may differ from the reference program's by a relative error of at most 0.0001.
Values sent between devices are 32-bit elements; how exact they have to be, the bound alone decides.
No kernel may reach another device: no remote copies, remote signals or barrier semaphores. Data moves between devices by JAX's collectives and lax.ppermute only.
A program may use at most 64 MiB of HBM per device.

```python
import math
import jax
import jax.numpy as jnp
from jax import lax

LON_DEV = 8
PARALLEL_TOTAL = 128
VERTICAL_LAYERS = 64
NTR = 16
STEPS = 2
SUBS = 2
TILES = 16
MERIDIAN_TOTAL = 128
CTILE = 1024
CPAIR = 64
COLUMNS = 16384


def draw_profile_block_order(key, part):
    key = jax.random.fold_in(key, 7)
    keys = jax.random.split(key, TILES)
    orders = jax.vmap(lambda single: jax.random.permutation(single, CTILE))(keys).astype(jnp.int32)
    tile_ids = jnp.arange(TILES, dtype=jnp.int32)[:, None]
    ranks = jnp.zeros((TILES, CTILE), jnp.int32).at[tile_ids, orders].set(jnp.broadcast_to(jnp.arange(CTILE, dtype=jnp.int32)[None, :], (TILES, CTILE)))
    block_offsets = ranks // CPAIR * CTILE + tile_ids * CPAIR + ranks % CPAIR
    return block_offsets.reshape(TILES * LON_DEV, PARALLEL_TOTAL)


def place_ends(array, key, least, top_value):
    place = [jax.random.randint(jax.random.fold_in(key, axis), (), 0, length) for axis, length in enumerate(array.shape)]
    longest = array.shape.index(max(array.shape))
    neighbour = place[:longest] + [(place[longest] + 1) % array.shape[longest]] + place[longest + 1:]
    return array.at[tuple(place)].set(least).at[tuple(neighbour)].set(top_value)


def level_of(key, extent, cuts, low, largest):
    def one(dim, parts):
        draws = jax.random.uniform(jax.random.fold_in(jax.random.fold_in(key, 6), dim), (parts,), jnp.float32, low / len(cuts), largest / len(cuts))
        return jnp.repeat(jnp.exp(draws), extent[dim] // parts).reshape((-1,) + (1,) * (len(extent) - dim - 1))

    gain = one(*cuts[0])
    for cut in cuts[1:]:
        gain = gain * one(*cut)
    return gain


def bell_draw(stream_key, shape, spread, most, pieces=(), kind=jnp.bfloat16):
    entries = spread * jax.random.normal(stream_key, shape, jnp.float32)
    if pieces:
        entries = entries * level_of(stream_key, shape, pieces, -0.22, 0.18)
    return jnp.clip(entries, -most, most).astype(kind)


def setup_inputs(seed: int = 0, part: int = 0) -> dict:
    key_of = jax.random.split(jax.random.key(seed), 10)
    own_keys = jax.random.split(jax.random.fold_in(key_of[9], part), 10)
    zonal_current = bell_draw(own_keys[0], (VERTICAL_LAYERS, MERIDIAN_TOTAL, PARALLEL_TOTAL), 0.5, 3.0, ((1, 16),), jnp.float32)
    meridional_current = bell_draw(own_keys[1], (VERTICAL_LAYERS, MERIDIAN_TOTAL, PARALLEL_TOTAL), 0.5, 3.0, ((1, 16),), jnp.float32)
    thermal_anomaly = bell_draw(own_keys[2], (VERTICAL_LAYERS, MERIDIAN_TOTAL, PARALLEL_TOTAL), 1.0, 5.0, ((1, 16),), jnp.float32)
    saltiness_anomaly = bell_draw(own_keys[3], (VERTICAL_LAYERS, MERIDIAN_TOTAL, PARALLEL_TOTAL), 1.0, 5.0, ((1, 16),), jnp.float32)
    species_amounts = bell_draw(own_keys[4], (NTR, VERTICAL_LAYERS, COLUMNS), 1.0, 5.0, ((2, 16),), jnp.float32)
    wet_layer_number = place_ends(jax.random.randint(own_keys[5], (MERIDIAN_TOTAL, PARALLEL_TOTAL), 0, VERTICAL_LAYERS + 1), jax.random.fold_in(own_keys[5], 1), 0, VERTICAL_LAYERS).astype(jnp.int32)
    profile_block_order = draw_profile_block_order(jax.random.fold_in(jax.random.fold_in(key_of[9], part), 71), part)
    species_coupling = bell_draw(key_of[7], (NTR, NTR), NTR ** -0.5, 1.5, (), jnp.float32)
    settling_fraction = jnp.clip(jnp.exp(jax.random.uniform(key_of[8], (NTR,), jnp.float32, math.log(0.05), math.log(0.5))), 0.05, 0.5)
    return {"zonal_current": zonal_current, "meridional_current": meridional_current, "thermal_anomaly": thermal_anomaly, "saltiness_anomaly": saltiness_anomaly, "species_amounts": species_amounts, "wet_layer_number": wet_layer_number, "profile_block_order": profile_block_order, "species_coupling": species_coupling, "settling_fraction": settling_fraction}


def pad_lat(field):
    return jnp.pad(field, ((0, 0), (0, 0), (1, 1)))


def tile_step(extended, thermal_forcing, mask, fcor):
    u_ext, v_ext, t_ext, s_ext = extended[0], extended[1], extended[2], extended[3]
    pressure = 0.1 * jnp.cumsum(-0.2 * t_ext + 0.8 * s_ext, axis=0)

    def centre(field):
        return field[:, 1:-1, :]

    def diff_x(field):
        return 0.5 * (field[:, 2:, :] - field[:, :-2, :])

    def diff_y(field):
        padded = pad_lat(centre(field))
        return 0.5 * (padded[:, :, 2:] - padded[:, :, :-2])

    def laplace(field):
        padded = pad_lat(centre(field))
        return field[:, 2:, :] + field[:, :-2, :] + padded[:, :, 2:] + padded[:, :, :-2] - 4.0 * centre(field)

    u_now, v_now, t_now, s_now = centre(u_ext), centre(v_ext), centre(t_ext), centre(s_ext)
    new_u = mask * (u_now + 0.2 * (fcor * v_now - diff_x(pressure) + 0.1 * laplace(u_ext)))
    new_v = mask * (v_now + 0.2 * (-fcor * u_now - diff_y(pressure) + 0.1 * laplace(v_ext)))
    new_t = mask * (t_now + 0.2 * (-(u_now * diff_x(t_ext) + v_now * diff_y(t_ext)) + 0.1 * laplace(t_ext) + thermal_forcing))
    new_s = mask * (s_now + 0.2 * (-(u_now * diff_x(s_ext) + v_now * diff_y(s_ext)) + 0.1 * laplace(s_ext)))
    return new_u, new_v, new_t, new_s


def tracer_step(species_amounts, temp_patch, depth_patch, species_coupling, settling_fraction):
    layer_total = species_amounts.shape[1]
    level_ids = jnp.arange(layer_total, dtype=jnp.float32)[:, None]
    pmask = (level_ids < depth_patch[None, :]).astype(jnp.float32)
    below = jnp.concatenate([pmask[1:], jnp.zeros_like(pmask[:1])], axis=0)
    chloro = species_amounts[0]
    trans = jnp.exp(-jnp.cumsum((0.5 + 0.1 * chloro * chloro) / layer_total, axis=0))
    above = jnp.concatenate([jnp.ones_like(trans[:1]), trans[:-1]], axis=0)
    thermal_forcing = layer_total * (above - trans) * pmask
    reacted = jnp.einsum("ij,jkc->ikc", species_coupling, species_amounts, precision=lax.Precision.HIGHEST)
    growth = jnp.exp(0.15 * temp_patch) * trans
    species_amounts = species_amounts + 0.2 * growth[None] * reacted
    for sub in range(SUBS):
        flux = settling_fraction[:, None, None] * species_amounts * below[None]
        moved = jnp.concatenate([jnp.zeros_like(flux[:, :1]), flux[:, :-1]], axis=1)
        species_amounts = species_amounts - flux + moved
    return species_amounts * pmask[None], thermal_forcing


def reference(zonal_current, meridional_current, thermal_anomaly, saltiness_anomaly, species_amounts, wet_layer_number, profile_block_order, species_coupling, settling_fraction):
    layer_total = thermal_anomaly.shape[0]
    block_offsets = profile_block_order.reshape(-1).astype(jnp.int32)
    mask = (jnp.arange(layer_total, dtype=jnp.int32)[:, None, None] < wet_layer_number[None]).astype(jnp.float32)
    lat = jnp.arange(PARALLEL_TOTAL, dtype=jnp.float32)
    fcor = 0.8 * jnp.sin(jnp.pi * (lat + 0.5) / PARALLEL_TOTAL - jnp.pi / 2)
    depth_flat = wet_layer_number.reshape(-1).astype(jnp.float32)
    depth_patch = jnp.zeros_like(depth_flat).at[block_offsets].set(depth_flat)
    prognostic_arrays = (zonal_current, meridional_current, thermal_anomaly, saltiness_anomaly)
    for step in range(STEPS):
        temp_flat = prognostic_arrays[2].reshape(layer_total, -1)
        temp_patch = jnp.zeros_like(temp_flat).at[:, block_offsets].set(temp_flat)
        species_amounts, block_thermal_forcing = tracer_step(species_amounts, temp_patch, depth_patch, species_coupling, settling_fraction)
        thermal_forcing = block_thermal_forcing[:, block_offsets].reshape(thermal_anomaly.shape)
        stacked = jnp.stack(prognostic_arrays)
        extended = jnp.concatenate([stacked[:, :, -1:], stacked, stacked[:, :, :1]], axis=2)
        prognostic_arrays = tile_step(extended, thermal_forcing, mask, fcor)
    return prognostic_arrays[0], prognostic_arrays[1], prognostic_arrays[2], prognostic_arrays[3], species_amounts
```

```python
import jax
import jax.numpy as jnp
from jax import lax
from jax.experimental import pallas as pl
from jax.experimental.pallas import tpu as pltpu
from jax.sharding import PartitionSpec as P

SUBS = 2
AXES = ("cols", "comp")
F32 = jnp.float32
BF16 = jnp.bfloat16
MIB = 1024 * 1024
BLOCK = 256


def split(x):
    hi = x.astype(BF16)
    return hi, (x - hi.astype(F32)).astype(BF16)


def split3(x):
    hi = x.astype(BF16)
    rest = x - hi.astype(F32)
    mid = rest.astype(BF16)
    return hi, mid, (rest - mid.astype(F32)).astype(BF16)


def mxu(a, b):
    return jnp.dot(a, b, preferred_element_type=F32)


def iota(shape, dim):
    return lax.broadcasted_iota(jnp.int32, shape, dim)


def pack(out_ref, row, x, cpair):
    groups = 128 // cpair
    rows = x.shape[0] // groups
    lane_group = iota((rows, 128), 1) // cpair
    for e in range(x.shape[1] // 128):
        part = x[:, e * 128 : (e + 1) * 128]
        for o in range(groups):
            out = None
            for g in range(groups):
                piece = part[g * rows : (g + 1) * rows]
                shift = (g - o) * cpair % 128
                if shift:
                    piece = pltpu.roll(piece, shift, 1)
                out = piece if out is None else jnp.where(lane_group == g, piece, out)
            out_ref[e * groups + o, row : row + rows, :] = out


def unpack(in_ref, row, rows, cpair, first, blocks):
    groups = 128 // cpair
    lane_group = iota((rows, 128), 1) // cpair
    columns = []
    for e in range(blocks):
        levels = []
        for g in range(groups):
            out = None
            for o in range(groups):
                piece = in_ref[first + e * groups + o, row : row + rows, :]
                shift = (o - g) * cpair % 128
                if shift:
                    piece = pltpu.roll(piece, shift, 1)
                out = piece if out is None else jnp.where(lane_group == o, piece, out)
            levels.append(out)
        columns.append(jnp.concatenate(levels, axis=0))
    return jnp.concatenate(columns, axis=1)


def light(chloro):
    levels = chloro.shape[0]
    absorbed = (0.5 + 0.1 * chloro * chloro) * (1.0 / levels)
    lower = (iota((levels, levels), 1) <= iota((levels, levels), 0)).astype(F32).astype(BF16)
    total = mxu(jnp.concatenate([lower] * 3, axis=1), jnp.concatenate(split3(absorbed), axis=0))
    trans = jnp.exp(-total)
    above = jnp.where(iota(trans.shape, 0) == 0, 1.0, pltpu.roll(trans, 1, 0))
    return trans, levels * (above - trans)


def sink(amounts, fraction):
    for _ in range(SUBS):
        flux = fraction * amounts
        amounts = amounts - flux + pltpu.roll(flux, 1, 0)
    return amounts


def split_kron(coupling):
    return jnp.concatenate(split(coupling), axis=0)


def mix(kron2, kron_hi, tracers):
    rows = tracers.shape[0]
    hi, lo = split(tracers)
    both = mxu(kron2, hi)
    return both[:rows] + both[rows:] + mxu(kron_hi, lo)


def start_kernel(cpair, order_ref, depth_ref, temp_ref, species_ref, pay_ref, place_ref, heat_ref, trans_ref, lhs, temp, chloro, sems):
    levels, lons, lats = temp_ref.shape
    ctile = lons * lats
    copies = [
        pltpu.make_async_copy(species_ref.at[0], chloro, sems.at[0]),
        pltpu.make_async_copy(temp_ref, temp, sems.at[1]),
    ]
    for copy in copies:
        copy.start()
    order = order_ref[...]
    bucket = (order >> (ctile.bit_length() - 1)) * cpair + (order & (cpair - 1))
    across = bucket.astype(F32).T.astype(jnp.int32)
    target = iota((lats, ctile), 1)
    for r in range(lons):
        place_ref[r * lats : (r + 1) * lats, :] = jnp.where(target == across[:, r : r + 1], 1.0, 0.0).astype(BF16)
    depth = depth_ref[...].astype(F32)
    copies[0].wait()
    trans, heat = light(chloro[...])
    heat_ref[...] = heat
    trans_ref[...] = trans
    rows = levels * cpair // 128
    pack(pay_ref, rows, heat, cpair)
    copies[1].wait()
    for r in range(lons):
        hi, lo = split(temp[:, r, :])
        at = slice(r * lats, (r + 1) * lats)
        lhs[0:levels, at] = hi
        lhs[levels : 2 * levels, at] = lo
        lhs[2 * levels : 2 * levels + 16, at] = jnp.broadcast_to(depth[r : r + 1], (16, lats)).astype(BF16)
    sent = mxu(lhs[...], place_ref[...])
    pack(pay_ref, 0, sent[0:levels] + sent[levels : 2 * levels], cpair)
    deep = sent[2 * levels : 2 * levels + 8]
    for d in range(pay_ref.shape[0]):
        e, o = divmod(d * cpair, 128)
        part = deep[:, e * 128 : (e + 1) * 128]
        pay_ref[d, 2 * rows : 2 * rows + 8, :] = pltpu.roll(part, 128 - o, 1) if o else part


def react_kernel(species_ref, trans_ref, kron_ref, out_ref):
    tracers, levels, columns = species_ref.shape
    span = kron_ref.shape[0] // tracers
    kron2 = split_kron(kron_ref[...])
    for k in range(0, levels, span):
        mixed = mix(kron2, kron2[: span * tracers], species_ref[:, k : k + span, :].reshape(span * tracers, columns))
        out_ref[:, k : k + span, :] = mixed.reshape(tracers, span, columns) * (0.2 * trans_ref[k : k + span, :])[None]


def tile_levels(fields, left_ref, right_ref, depth_ref, fcor_ref, outs):
    levels, lons, lats = fields[0].shape
    shape = (lons, lats)
    lon, lat = iota(shape, 0), iota(shape, 1)
    first_lon, last_lon, first_lat, last_lat = lon == 0, lon == lons - 1, lat == 0, lat == lats - 1
    depth = depth_ref[...]
    turn = jnp.broadcast_to(0.2 * fcor_ref[...], shape)

    def neighbours(f, lower, upper):
        return (
            jnp.where(first_lon, lower, pltpu.roll(f, 1, 0)),
            jnp.where(last_lon, upper, pltpu.roll(f, lons - 1, 0)),
            jnp.where(first_lat, 0.0, pltpu.roll(f, 1, 1)),
            jnp.where(last_lat, 0.0, pltpu.roll(f, lats - 1, 1)),
        )

    def eight(i, carry):
        at = pl.ds(pl.multiple_of(i * 8, 8), 8)
        lefts = [left_ref[n, at, :] for n in range(4)]
        rights = [right_ref[n, at, :] for n in range(4)]
        for j in range(8):
            k = i * 8 + j
            u, v, t, s = (f[k] for f in fields)
            lu, lv, lt, ls = (jnp.broadcast_to(x[j : j + 1], shape) for x in lefts)
            ru, rv, rt, rs = (jnp.broadcast_to(x[j : j + 1], shape) for x in rights)
            load, load_left, load_right = carry
            load = load + (0.8 * s - 0.2 * t)
            load_left = load_left + (0.8 * ls - 0.2 * lt)
            load_right = load_right + (0.8 * rs - 0.2 * rt)
            carry = (load, load_left, load_right)
            wet = k < depth
            p0, p1, p2, p3 = neighbours(load, load_left, load_right)
            u0, u1, u2, u3 = neighbours(u, lu, ru)
            v0, v1, v2, v3 = neighbours(v, lv, rv)
            t0, t1, t2, t3 = neighbours(t, lt, rt)
            s0, s1, s2, s3 = neighbours(s, ls, rs)
            half_u, half_v = 0.1 * u, 0.1 * v
            new_u = 0.92 * u + turn * v - 0.01 * (p1 - p0) + 0.02 * ((u0 + u1) + (u2 + u3))
            new_v = 0.92 * v - turn * u - 0.01 * (p3 - p2) + 0.02 * ((v0 + v1) + (v2 + v3))
            new_t = 0.92 * t - half_u * (t1 - t0) - half_v * (t3 - t2) + 0.02 * ((t0 + t1) + (t2 + t3))
            new_s = 0.92 * s - half_u * (s1 - s0) - half_v * (s3 - s2) + 0.02 * ((s0 + s1) + (s2 + s3))
            for out, new in zip(outs, (new_u, new_v, new_t, new_s)):
                out[k] = jnp.where(wet, new, 0.0)
        return carry

    zero = jnp.zeros(shape, F32)
    lax.fori_loop(0, levels // 8, eight, (zero, zero, zero))


def first_tile_kernel(cpair, u_ref, v_ref, t_ref, s_ref, left_ref, right_ref, depth_ref, fcor_ref, order_ref, place_ref,
                      out_u, out_v, out_t, out_s, pay_ref, back_ref, lhs):
    levels, lons, lats = t_ref.shape
    ctile = lons * lats
    tile_levels((u_ref, v_ref, t_ref, s_ref), left_ref, right_ref, depth_ref, fcor_ref, (out_u, out_v, out_t, out_s))
    for r in range(lons):
        at = slice(r * lats, (r + 1) * lats)
        lhs[0:levels, at], lhs[levels : 2 * levels, at] = split(out_t[:, r, :])
    sent = mxu(lhs[...], place_ref[...])
    pack(pay_ref, 0, sent[0:levels] + sent[levels : 2 * levels], cpair)
    order = order_ref[...]
    bucket = (order >> (ctile.bit_length() - 1)) * cpair + (order & (cpair - 1))
    source = iota((ctile, lats), 0)
    for r in range(lons):
        back_ref[:, r * lats : (r + 1) * lats] = jnp.where(source == bucket[r : r + 1], 1.0, 0.0).astype(BF16)


def chloro_kernel(cpair, recv_ref, react_ref, species_ref, settling_ref, xpay_ref, pay_ref, warm_ref, depth_ref, trans_ref, react, chloro, sems):
    levels, columns = warm_ref.shape
    rows = levels * cpair // 128
    copies = [
        pltpu.make_async_copy(species_ref.at[0], chloro, sems.at[0]),
        pltpu.make_async_copy(react_ref.at[0], react, sems.at[1]),
    ]
    for copy in copies:
        copy.start()
    groups = 128 // cpair
    lane_group = iota((8, 128), 1) // cpair
    for e in range(columns // 128):
        out = None
        for o in range(groups):
            piece = recv_ref[e * groups + o, 2 * rows : 2 * rows + 8, :]
            if o:
                piece = pltpu.roll(piece, o * cpair, 1)
            out = piece if out is None else jnp.where(lane_group == o, piece, out)
        depth_ref[:, e * 128 : (e + 1) * 128] = out
    pay_ref[:, 0:rows, :] = xpay_ref[...]
    warm = jnp.exp(0.15 * unpack(recv_ref, 0, rows, cpair, 0, columns // 128))
    warm_ref[...] = warm
    level = iota((levels, columns), 0).astype(F32)
    depth = depth_ref[0:1, :]
    for copy in copies:
        copy.wait()
    amounts = chloro[...] + warm * react[...]
    amounts = sink(amounts, jnp.where(level + 1.0 < depth, settling_ref[0], 0.0))
    trans, heat = light(jnp.where(level < depth, amounts, 0.0))
    trans_ref[...] = trans
    pack(pay_ref, rows, heat, cpair)


def tracer_kernel(species_ref, react_ref, warm_ref, trans_ref, heat_ref, depth_ref, kron_ref, settling_ref, out_ref, next_ref):
    tracers, levels, columns = species_ref.shape
    level = iota((levels, columns), 0).astype(F32)
    depth = depth_ref[0:1, :]
    wet, below = level < depth, level + 1.0 < depth
    warm = warm_ref[...]
    for n in range(tracers):
        amounts = sink(species_ref[n] + warm * react_ref[n], jnp.where(below, settling_ref[n], 0.0))
        out_ref[n] = jnp.where(wet, amounts, 0.0)
    growth = 0.2 * trans_ref[...] * jnp.exp(0.03 * jnp.where(wet, heat_ref[...], 0.0))
    span = kron_ref.shape[0] // tracers
    kron2 = split_kron(kron_ref[...])
    for k in range(0, levels, span):
        mixed = mix(kron2, kron2[: span * tracers], out_ref[:, k : k + span, :].reshape(span * tracers, columns))
        next_ref[:, k : k + span, :] = mixed.reshape(tracers, span, columns) * growth[k : k + span][None]


def heat_kernel(cpair, recv_ref, back_ref, x_ref, depth_ref, u_ref, v_ref, s_ref, out_t, left_ref, right_ref):
    levels, lons, lats = x_ref.shape
    rows = levels * cpair // 128
    ctile = lons * lats
    heat = unpack(recv_ref, rows, rows, cpair, 0, ctile // 128)
    placed = mxu(jnp.concatenate(split(heat), axis=0), back_ref[...])
    placed = 0.2 * (placed[:levels] + placed[levels:])
    level = iota((levels, lats), 0)
    for r in range(lons):
        part = placed[:, r * lats : (r + 1) * lats]
        out_t[:, r, :] = x_ref[:, r, :] + jnp.where(level < depth_ref[r : r + 1, :], part, 0.0)
    for n, field in enumerate((u_ref, v_ref, out_t, s_ref)):
        left_ref[n] = field[:, 0, :]
        right_ref[n] = field[:, lons - 1, :]


def second_tile_kernel(u_ref, v_ref, t_ref, s_ref, left_ref, right_ref, depth_ref, fcor_ref, out_u, out_v, out_t, out_s):
    tile_levels((u_ref, v_ref, t_ref, s_ref), left_ref, right_ref, depth_ref, fcor_ref, (out_u, out_v, out_t, out_s))


def final_kernel(cpair, species_ref, react_ref, depth_ref, settling_ref, xrecv_ref, recv_ref, back_ref, wet_ref, part_ref, out_ref, out_t, heat):
    step = pl.program_id(0)
    tracers, levels, columns = species_ref.shape
    _, lons, lats = part_ref.shape
    rows = levels * cpair // 128

    @pl.when(step == 0)
    def _():
        heat[0:levels, :], heat[levels : 2 * levels, :] = split(unpack(recv_ref, rows, rows, cpair, 0, lons * lats // 128))
        out_t[...] = part_ref[...]

    warm = jnp.exp(0.15 * unpack(xrecv_ref, 0, rows, cpair, 0, columns // 128))
    level = iota((levels, columns), 0).astype(F32)
    depth = depth_ref[0:1, :]
    wet, below = level < depth, level + 1.0 < depth
    for n in range(tracers):
        amounts = sink(species_ref[n] + warm * react_ref[n], jnp.where(below, settling_ref[n], 0.0))
        out_ref[n] = jnp.where(wet, amounts, 0.0)
    placed = mxu(heat[...], back_ref[...])
    placed = 0.2 * (placed[:levels] + placed[levels:])
    tile_level = iota((levels, lats), 0)
    share = columns // lats
    for i in range(lons // share):

        @pl.when(step == i)
        def _():
            for r in range(share):
                lon = i * share + r
                part = placed[:, r * lats : (r + 1) * lats]
                out_t[:, lon, :] = part_ref[:, lon, :] + jnp.where(tile_level < wet_ref[lon : lon + 1, :], part, 0.0)


def whole(count):
    return [pl.BlockSpec(memory_space=pltpu.VMEM)] * count


ANY = pl.BlockSpec(memory_space=pl.ANY)
SMEM = pl.BlockSpec(memory_space=pltpu.SMEM)


def params(mib=48):
    return pltpu.CompilerParams(vmem_limit_bytes=mib * MIB)


def cost(flops, moved):
    return pl.CostEstimate(flops=flops, bytes_accessed=moved, transcendentals=0)


def shape(*dims, dtype=F32):
    return jax.ShapeDtypeStruct(dims, dtype)


def halo(left_edge, right_edge):
    count = lax.axis_size(AXES)
    ahead = [(i, (i + 1) % count) for i in range(count)]
    return lax.ppermute(right_edge, AXES, ahead), lax.ppermute(left_edge, AXES, [(b, a) for a, b in ahead])


def exchange(pay):
    return lax.all_to_all(pay, AXES, split_axis=0, concat_axis=0, tiled=True)


def body(u, v, temp, salt, species, wet_layers, order, coupling, settling):
    levels, lons, lats = temp.shape
    tracers, _, ctile = species.shape
    tiles = lax.axis_size(AXES)
    cpair = ctile // tiles
    rows = levels * cpair // 128
    field = shape(levels, lons, lats)
    column = shape(levels, ctile)
    edge = shape(4, levels, lats)
    onehot = shape(ctile, ctile, dtype=BF16)
    fcor = (0.8 * jnp.sin(jnp.pi * (jnp.arange(lats, dtype=F32) + 0.5) / lats - jnp.pi / 2))[None]
    kron = jnp.kron(coupling, jnp.eye(256 // tracers, dtype=F32))

    pay, place, heat1, trans1 = pl.pallas_call(
        lambda *refs: start_kernel(cpair, *refs),
        out_shape=[shape(tiles, 2 * rows + 8, 128), onehot, column, column],
        in_specs=whole(2) + [ANY, ANY],
        out_specs=whole(4),
        scratch_shapes=[
            pltpu.VMEM((2 * levels + 16, ctile), BF16),
            pltpu.VMEM((levels, lons, lats), F32),
            pltpu.VMEM((levels, ctile), F32),
            pltpu.SemaphoreType.DMA((2,)),
        ],
        compiler_params=params(),
        name="start",
    )(order, wet_layers, temp, species)
    recv_a = exchange(pay)

    stacked = jnp.stack([u, v, temp, salt])
    left, right = halo(stacked[:, :, 0], stacked[:, :, lons - 1])
    grid = (ctile // BLOCK,)
    tracer_block = pl.BlockSpec((tracers, levels, BLOCK), lambda i: (0, 0, i))
    column_block = pl.BlockSpec((levels, BLOCK), lambda i: (0, i))
    kron_block = pl.BlockSpec((256, 256), lambda i: (0, 0))
    mix_flops = 6 * 256 * levels * tracers * ctile
    react1 = pl.pallas_call(
        react_kernel,
        grid=grid,
        out_shape=shape(tracers, levels, ctile),
        in_specs=[tracer_block, column_block, kron_block],
        out_specs=tracer_block,
        compiler_params=params(),
        cost_estimate=cost(mix_flops, 8 * MIB),
        name="react",
    )(species, trans1, kron)
    u1, v1, x0, s1, xpay, back = pl.pallas_call(
        lambda *refs: first_tile_kernel(cpair, *refs),
        out_shape=[field] * 4 + [shape(tiles, rows, 128), onehot],
        in_specs=whole(10),
        out_specs=whole(6),
        scratch_shapes=[pltpu.VMEM((2 * levels, ctile), BF16)],
        compiler_params=params(),
        cost_estimate=cost(4 * levels * ctile * ctile, 8 * MIB),
        name="tile_one",
    )(u, v, temp, salt, left, right, wet_layers, fcor, order, place)

    pay, warm, depth, trans2 = pl.pallas_call(
        lambda *refs: chloro_kernel(cpair, *refs),
        out_shape=[shape(tiles, 2 * rows, 128), column, shape(8, ctile), column],
        in_specs=whole(1) + [ANY, ANY, SMEM] + whole(1),
        out_specs=whole(4),
        scratch_shapes=[
            pltpu.VMEM((levels, ctile), F32),
            pltpu.VMEM((levels, ctile), F32),
            pltpu.SemaphoreType.DMA((2,)),
        ],
        compiler_params=params(),
        name="chloro",
    )(recv_a, react1, species, settling, xpay)
    recv_b = exchange(pay)

    recv_a, _ = lax.optimization_barrier((recv_a, pay))
    t1, left_edge, right_edge = pl.pallas_call(
        lambda *refs: heat_kernel(cpair, *refs),
        out_shape=[field, edge, edge],
        in_specs=whole(7),
        out_specs=whole(3),
        compiler_params=params(),
        cost_estimate=cost(4 * levels * ctile * ctile, 4 * MIB),
        name="heat",
    )(recv_a, back, x0, wet_layers, u1, v1, s1)
    left, right = halo(left_edge, right_edge)
    species1, react2 = pl.pallas_call(
        tracer_kernel,
        grid=grid,
        out_shape=[shape(tracers, levels, ctile)] * 2,
        in_specs=[tracer_block, tracer_block] + [column_block] * 3 + [pl.BlockSpec((8, BLOCK), lambda i: (0, i)), kron_block, SMEM],
        out_specs=[tracer_block] * 2,
        compiler_params=params(),
        cost_estimate=cost(mix_flops, 16 * MIB),
        name="tracer",
    )(species, react1, warm, trans2, heat1, depth, kron, settling)
    u2, v2, t2, s2 = pl.pallas_call(
        second_tile_kernel,
        out_shape=[field] * 4,
        in_specs=whole(8),
        out_specs=whole(4),
        compiler_params=params(),
        cost_estimate=cost(60 * levels * ctile, 2 * MIB),
        name="tile_two",
    )(u1, v1, t1, s1, left, right, wet_layers, fcor)

    field_block = pl.BlockSpec((levels, lons, lats), lambda i: (0, 0, 0))
    species2, t2 = pl.pallas_call(
        lambda *refs: final_kernel(cpair, *refs),
        grid=grid,
        out_shape=[shape(tracers, levels, ctile), field],
        in_specs=[
            tracer_block,
            tracer_block,
            pl.BlockSpec((8, BLOCK), lambda i: (0, i)),
            SMEM,
            pl.BlockSpec((BLOCK // cpair, 2 * rows, 128), lambda i: (i, 0, 0)),
            pl.BlockSpec((tiles, 2 * rows, 128), lambda i: (0, 0, 0)),
            pl.BlockSpec((ctile, BLOCK), lambda i: (0, i)),
            pl.BlockSpec((lons, lats), lambda i: (0, 0)),
            field_block,
        ],
        out_specs=[tracer_block, field_block],
        scratch_shapes=[pltpu.VMEM((2 * levels, ctile), BF16)],
        compiler_params=params(),
        name="final",
    )(species1, react2, depth, settling, recv_b, recv_b, back, wet_layers, t2)
    return u2, v2, t2, s2, species2


def solution(mesh):
    tile = P(None, ("groups", "cols", "comp"), None)
    patch = P(None, None, ("groups", "cols", "comp"))
    index = P(("groups", "cols", "comp"), None)
    return jax.shard_map(
        body,
        mesh=mesh,
        in_specs=(tile, tile, tile, tile, patch, index, index, P(), P()),
        out_specs=(tile, tile, tile, tile, patch),
        check_vma=False,
    )
```

```python
import jax
import jax.numpy as jnp
from jax import lax
from jax.experimental import pallas as pl
from jax.experimental.pallas import tpu as pltpu
from jax.sharding import PartitionSpec as P

SUBS = 2
AXES = ("cols", "comp")
F32 = jnp.float32
BF16 = jnp.bfloat16
MIB = 1024 * 1024
BLOCK = 256


def split(x):
    hi = x.astype(BF16)
    return hi, (x - hi.astype(F32)).astype(BF16)


def split3(x):
    hi = x.astype(BF16)
    rest = x - hi.astype(F32)
    mid = rest.astype(BF16)
    return hi, mid, (rest - mid.astype(F32)).astype(BF16)


def mxu(a, b):
    return jnp.dot(a, b, preferred_element_type=F32)


def iota(shape, dim):
    return lax.broadcasted_iota(jnp.int32, shape, dim)


def pack(out_ref, row, x, cpair):
    groups = 128 // cpair
    rows = x.shape[0] // groups
    lane_group = iota((rows, 128), 1) // cpair
    for e in range(x.shape[1] // 128):
        part = x[:, e * 128 : (e + 1) * 128]
        for o in range(groups):
            out = None
            for g in range(groups):
                piece = part[g * rows : (g + 1) * rows]
                shift = (g - o) * cpair % 128
                if shift:
                    piece = pltpu.roll(piece, shift, 1)
                out = piece if out is None else jnp.where(lane_group == g, piece, out)
            out_ref[e * groups + o, row : row + rows, :] = out


def unpack(in_ref, row, rows, cpair, first, blocks):
    groups = 128 // cpair
    lane_group = iota((rows, 128), 1) // cpair
    columns = []
    for e in range(blocks):
        levels = []
        for g in range(groups):
            out = None
            for o in range(groups):
                piece = in_ref[first + e * groups + o, row : row + rows, :]
                shift = (o - g) * cpair % 128
                if shift:
                    piece = pltpu.roll(piece, shift, 1)
                out = piece if out is None else jnp.where(lane_group == o, piece, out)
            levels.append(out)
        columns.append(jnp.concatenate(levels, axis=0))
    return jnp.concatenate(columns, axis=1)


def light(chloro):
    levels = chloro.shape[0]
    absorbed = (0.5 + 0.1 * chloro * chloro) * (1.0 / levels)
    lower = (iota((levels, levels), 1) <= iota((levels, levels), 0)).astype(F32).astype(BF16)
    total = mxu(jnp.concatenate([lower] * 3, axis=1), jnp.concatenate(split3(absorbed), axis=0))
    trans = jnp.exp(-total)
    above = jnp.where(iota(trans.shape, 0) == 0, 1.0, pltpu.roll(trans, 1, 0))
    return trans, levels * (above - trans)


def sink(amounts, fraction):
    for _ in range(SUBS):
        flux = fraction * amounts
        amounts = amounts - flux + pltpu.roll(flux, 1, 0)
    return amounts


def split_kron(coupling, span):
    tracers = coupling.shape[0]
    size = tracers * span
    tall = (iota((size, tracers), 0) // span == iota((size, tracers), 1)).astype(F32).astype(BF16)
    wide = (iota((tracers, size), 1) // span == iota((tracers, size), 0)).astype(F32).astype(BF16)
    same = iota((size, size), 0) % span == iota((size, size), 1) % span
    terms = [jnp.where(same, mxu(mxu(tall, term).astype(BF16), wide), 0.0).astype(BF16) for term in split(coupling)]
    return jnp.concatenate(terms, axis=0)


def mix(kron_ref, tracers):
    rows = tracers.shape[0]
    hi, lo = split(tracers)
    both = mxu(kron_ref[...], hi)
    return both[:rows] + both[rows:] + mxu(kron_ref[:rows, :], lo)


def mix_levels(kron_ref, tracers_ref, scale_ref, out_ref, k):
    tracers, _, columns = tracers_ref.shape
    size = kron_ref.shape[1]
    span = size // tracers

    def block(i, _):
        at = pl.ds(pl.multiple_of(i * BLOCK, BLOCK), BLOCK)
        mixed = mix(kron_ref, tracers_ref[:, k : k + span, at].reshape(size, BLOCK))
        out_ref[:, k : k + span, at] = mixed.reshape(tracers, span, BLOCK) * scale_ref[k : k + span, at][None]
        return 0

    lax.fori_loop(0, columns // BLOCK, block, 0)


def sink_all(species_ref, warm_ref, react_ref, depth_ref, settling_ref, wet, below, out_ref, before, after):
    tracers, levels, columns = species_ref.shape
    level = iota((levels, columns), 0).astype(F32)
    depth = depth_ref[0:1, :]
    wet[...] = jnp.where(level < depth, 1.0, 0.0)
    below[...] = jnp.where(level + 1.0 < depth, 1.0, 0.0)

    def one(n, _):
        before(n)
        fraction = settling_ref[n]
        for c in range(0, columns, 128):
            at = slice(c, c + 128)
            amounts = species_ref[n, :, at] + warm_ref[:, at] * react_ref[n, :, at]
            out_ref[n, :, at] = sink(amounts, fraction * below[:, at]) * wet[:, at]
        after(n)
        return 0

    lax.fori_loop(0, tracers, one, 0)


def place_columns(order, onehot, cpair):
    lons, lats = order.shape
    target = iota((lats, lons * lats), 1)
    across = buckets(order, cpair).astype(F32).T.astype(jnp.int32)
    for r in range(lons):
        onehot[r * lats : (r + 1) * lats, :] = jnp.where(target == across[:, r : r + 1], 1.0, 0.0).astype(BF16)


def buckets(order, cpair):
    ctile = order.shape[0] * order.shape[1]
    return (order >> (ctile.bit_length() - 1)) * cpair + (order & (cpair - 1))


def start_kernel(cpair, order_hbm, depth_hbm, temp_hbm, species_hbm, pay_hbm, scale_ref, heat_ref, order, depths, temp, chloro, pay, place, lhs, sems):
    levels, lons, lats = temp.shape
    copies = [
        pltpu.make_async_copy(src, dst, sems.at[i])
        for i, (src, dst) in enumerate(((order_hbm, order), (depth_hbm, depths), (species_hbm.at[0], chloro), (temp_hbm, temp)))
    ]
    for copy in copies:
        copy.start()
    rows = levels * cpair // 128
    copies[0].wait()
    place_columns(order[...], place, cpair)
    copies[1].wait()
    depth = depths[...].astype(F32)
    copies[2].wait()
    trans, heat = light(chloro[...])
    heat_ref[...] = heat
    scale_ref[...] = 0.2 * trans
    pack(pay, 0, heat, cpair)
    send_heat = pltpu.make_async_copy(pay.at[:, 0:rows], pay_hbm.at[:, 0:rows], sems.at[4])
    send_heat.start()
    copies[3].wait()
    for r in range(lons):
        hi, lo = split(temp[:, r, :])
        at = slice(r * lats, (r + 1) * lats)
        lhs[0:levels, at] = hi
        lhs[levels : 2 * levels, at] = lo
        lhs[2 * levels : 2 * levels + 16, at] = jnp.broadcast_to(depth[r : r + 1], (16, lats)).astype(BF16)
    sent = mxu(lhs[...], place[...])
    pack(pay, rows, sent[0:levels] + sent[levels : 2 * levels], cpair)
    deep = sent[2 * levels : 2 * levels + 8]
    for d in range(pay.shape[0]):
        e, o = divmod(d * cpair, 128)
        part = deep[:, e * 128 : (e + 1) * 128]
        pay[d, 2 * rows : 2 * rows + 8, :] = pltpu.roll(part, 128 - o, 1) if o else part
    send_temp = pltpu.make_async_copy(pay.at[:, rows : 2 * rows + 8], pay_hbm.at[:, rows : 2 * rows + 8], sems.at[5])
    send_temp.start()
    send_heat.wait()
    send_temp.wait()


def react_kernel(species_hbm, scale_ref, coupling_ref, react_hbm, first_ref, kron_ref, species, react, sems, out_sems):
    tracers, levels, columns = species.shape
    span = 256 // tracers
    parts = [slice(k, k + span) for k in range(0, levels, span)]
    copies = [pltpu.make_async_copy(species_hbm.at[:, at], species.at[:, at], sems.at[i]) for i, at in enumerate(parts)]
    sends = [pltpu.make_async_copy(react.at[:, at], react_hbm.at[:, at], out_sems.at[i]) for i, at in enumerate(parts)]
    for copy in copies:
        copy.start()
    kron_ref[...] = split_kron(coupling_ref[...], span)
    for copy, send, at in zip(copies, sends, parts):
        copy.wait()
        mix_levels(kron_ref, species, scale_ref, react, at.start)
        send.start()
    first_ref[0] = species[0]
    first_ref[1] = react[0]
    for send in sends:
        send.wait()


def tile_levels(fields, left_ref, right_ref, depth_ref, fcor_ref, outs):
    levels, lons, lats = fields[0].shape
    shape = (lons, lats)
    lon, lat = iota(shape, 0), iota(shape, 1)
    first_lon, last_lon, first_lat, last_lat = lon == 0, lon == lons - 1, lat == 0, lat == lats - 1
    depth = depth_ref[...]
    turn = jnp.broadcast_to(0.2 * fcor_ref[...], shape)

    def neighbours(f, lower, upper):
        return (
            jnp.where(first_lon, lower, pltpu.roll(f, 1, 0)),
            jnp.where(last_lon, upper, pltpu.roll(f, lons - 1, 0)),
            jnp.where(first_lat, 0.0, pltpu.roll(f, 1, 1)),
            jnp.where(last_lat, 0.0, pltpu.roll(f, lats - 1, 1)),
        )

    def eight(i, carry):
        at = pl.ds(pl.multiple_of(i * 8, 8), 8)
        lefts = [left_ref[n, at, :] for n in range(4)]
        rights = [right_ref[n, at, :] for n in range(4)]
        for j in range(8):
            k = i * 8 + j
            u, v, t, s = (f[k] for f in fields)
            lu, lv, lt, ls = (jnp.broadcast_to(x[j : j + 1], shape) for x in lefts)
            ru, rv, rt, rs = (jnp.broadcast_to(x[j : j + 1], shape) for x in rights)
            load, load_left, load_right = carry
            load = load + (0.8 * s - 0.2 * t)
            load_left = load_left + (0.8 * ls - 0.2 * lt)
            load_right = load_right + (0.8 * rs - 0.2 * rt)
            carry = (load, load_left, load_right)
            wet = k < depth
            p0, p1, p2, p3 = neighbours(load, load_left, load_right)
            u0, u1, u2, u3 = neighbours(u, lu, ru)
            v0, v1, v2, v3 = neighbours(v, lv, rv)
            t0, t1, t2, t3 = neighbours(t, lt, rt)
            s0, s1, s2, s3 = neighbours(s, ls, rs)
            half_u, half_v = 0.1 * u, 0.1 * v
            new_u = 0.92 * u + turn * v - 0.01 * (p1 - p0) + 0.02 * ((u0 + u1) + (u2 + u3))
            new_v = 0.92 * v - turn * u - 0.01 * (p3 - p2) + 0.02 * ((v0 + v1) + (v2 + v3))
            new_t = 0.92 * t - half_u * (t1 - t0) - half_v * (t3 - t2) + 0.02 * ((t0 + t1) + (t2 + t3))
            new_s = 0.92 * s - half_u * (s1 - s0) - half_v * (s3 - s2) + 0.02 * ((s0 + s1) + (s2 + s3))
            for out, new in zip(outs, (new_u, new_v, new_t, new_s)):
                out[k] = jnp.where(wet, new, 0.0)
        return carry

    zero = jnp.zeros(shape, F32)
    lax.fori_loop(0, levels // 8, eight, (zero, zero, zero))


def first_tile_kernel(cpair, u_ref, v_ref, t_ref, s_ref, left_ref, right_ref, depth_ref, fcor_ref, order_ref,
                      pay_hbm, out_u, out_v, out_t, out_s, pay, place, lhs, sem):
    levels, lons, lats = t_ref.shape
    rows = levels * cpair // 128
    tile_levels((u_ref, v_ref, t_ref, s_ref), left_ref, right_ref, depth_ref, fcor_ref, (out_u, out_v, out_t, out_s))
    place_columns(order_ref[...], place, cpair)
    for r in range(lons):
        at = slice(r * lats, (r + 1) * lats)
        lhs[0:levels, at], lhs[levels : 2 * levels, at] = split(out_t[:, r, :])
    sent = mxu(lhs[...], place[...])
    pack(pay, 0, sent[0:levels] + sent[levels : 2 * levels], cpair)
    send = pltpu.make_async_copy(pay, pay_hbm.at[:, 0:rows], sem.at[0])
    send.start()
    send.wait()


def chloro_kernel(cpair, recv_ref, settling_ref, first_ref, pay_in, pay_hbm, warm_ref, depth_ref, scale_ref, pay, sem):
    levels, columns = warm_ref.shape
    rows = levels * cpair // 128
    groups = 128 // cpair
    lane_group = iota((8, 128), 1) // cpair
    for e in range(columns // 128):
        out = None
        for o in range(groups):
            piece = recv_ref[e * groups + o, 2 * rows : 2 * rows + 8, :]
            if o:
                piece = pltpu.roll(piece, o * cpair, 1)
            out = piece if out is None else jnp.where(lane_group == o, piece, out)
        depth_ref[:, e * 128 : (e + 1) * 128] = out
    warm = jnp.exp(0.15 * unpack(recv_ref, rows, rows, cpair, 0, columns // 128))
    warm_ref[...] = warm
    level = iota((levels, columns), 0).astype(F32)
    depth = depth_ref[0:1, :]
    amounts = first_ref[0] + warm * first_ref[1]
    amounts = sink(amounts, jnp.where(level + 1.0 < depth, settling_ref[0], 0.0))
    trans, heat = light(jnp.where(level < depth, amounts, 0.0))
    scale_ref[...] = 0.2 * trans
    pack(pay, 0, heat, cpair)
    send = pltpu.make_async_copy(pay, pay_hbm.at[:, rows : 2 * rows], sem.at[0])
    send.start()
    send.wait()


def heat_kernel(cpair, recv_ref, order_ref, depth_ref, u_ref, v_ref, x_ref, s_ref, back_hbm, out_t, left_ref, right_ref, back, sem):
    levels, lons, lats = x_ref.shape
    rows = levels * cpair // 128
    ctile = lons * lats
    bucket = buckets(order_ref[...], cpair)
    source = iota((ctile, lats), 0)
    for r in range(lons):
        back[:, r * lats : (r + 1) * lats] = jnp.where(source == bucket[r : r + 1], 1.0, 0.0).astype(BF16)
    save = pltpu.make_async_copy(back, back_hbm, sem.at[0])
    save.start()
    heat = unpack(recv_ref, 0, rows, cpair, 0, ctile // 128)
    placed = mxu(jnp.concatenate(split(heat), axis=0), back[...])
    placed = 0.2 * (placed[:levels] + placed[levels:])
    level = iota((levels, lats), 0)
    for r in range(lons):
        part = placed[:, r * lats : (r + 1) * lats]
        out_t[:, r, :] = x_ref[:, r, :] + jnp.where(level < depth_ref[r : r + 1, :], part, 0.0)
    for n, field in enumerate((u_ref, v_ref, out_t, s_ref)):
        left_ref[n] = field[:, 0, :]
        right_ref[n] = field[:, lons - 1, :]
    save.wait()


def tracer_kernel(species_hbm, react_hbm, warm_ref, scale_ref, heat_ref, depth_ref, kron_ref, settling_ref, out_hbm, next_hbm,
                  species, react, wet, below, in_sems, out_sems, next_sems):
    tracers, levels, columns = species.shape
    span = 256 // tracers

    def fetch(n):
        return (
            pltpu.make_async_copy(species_hbm.at[n], species.at[n], in_sems.at[2 * n]),
            pltpu.make_async_copy(react_hbm.at[n], react.at[n], in_sems.at[2 * n + 1]),
        )

    def save(n):
        return pltpu.make_async_copy(species.at[n], out_hbm.at[n], out_sems.at[n])

    for n in range(tracers):
        for copy in fetch(n):
            copy.start()

    def before(n):
        for copy in fetch(n):
            copy.wait()

    sink_all(species, warm_ref, react, depth_ref, settling_ref, wet, below, species, before, lambda n: save(n).start())
    below[...] = scale_ref[...] * jnp.exp(0.03 * (wet[...] * heat_ref[...]))
    parts = [slice(k, k + span) for k in range(0, levels, span)]
    sends = [pltpu.make_async_copy(react.at[:, at], next_hbm.at[:, at], next_sems.at[i]) for i, at in enumerate(parts)]
    for send, at in zip(sends, parts):
        mix_levels(kron_ref, species, below, react, at.start)
        send.start()
    for n in range(tracers):
        save(n).wait()
    for send in sends:
        send.wait()


def second_tile_kernel(u_ref, v_ref, t_ref, s_ref, left_ref, right_ref, depth_ref, fcor_ref, out_u, out_v, out_t, out_s):
    tile_levels((u_ref, v_ref, t_ref, s_ref), left_ref, right_ref, depth_ref, fcor_ref, (out_u, out_v, out_t, out_s))


def final_kernel(cpair, species_hbm, react_hbm, back_hbm, depth_ref, settling_ref, recv_ref, wet_ref, part_ref, out_hbm, t_hbm,
                 species, react, back, t, warm, wet, below, in_sems, out_sems, sems):
    tracers, levels, columns = species.shape
    _, lons, lats = part_ref.shape
    rows = levels * cpair // 128

    def fetch(n):
        return (
            pltpu.make_async_copy(species_hbm.at[n], species.at[n], in_sems.at[2 * n]),
            pltpu.make_async_copy(react_hbm.at[n], react.at[n], in_sems.at[2 * n + 1]),
        )

    def send(n):
        return pltpu.make_async_copy(species.at[n], out_hbm.at[n], out_sems.at[n])

    for copy in fetch(0):
        copy.start()
    fetch_back = pltpu.make_async_copy(back_hbm, back, sems.at[0])
    fetch_back.start()
    for n in range(1, tracers):
        for copy in fetch(n):
            copy.start()

    def before(n):
        for copy in fetch(n):
            copy.wait()

    warm[...] = jnp.exp(0.15 * unpack(recv_ref, 0, rows, cpair, 0, columns // 128))
    heat = jnp.concatenate(split(unpack(recv_ref, rows, rows, cpair, 0, columns // 128)), axis=0)
    fetch_back.wait()
    placed = mxu(heat, back[...])
    placed = 0.2 * (placed[:levels] + placed[levels:])
    level = iota((levels, lats), 0)
    for r in range(lons):
        part = placed[:, r * lats : (r + 1) * lats]
        t[:, r, :] = part_ref[:, r, :] + jnp.where(level < wet_ref[r : r + 1, :], part, 0.0)
    send_t = pltpu.make_async_copy(t, t_hbm, sems.at[1])
    send_t.start()
    sink_all(species, warm, react, depth_ref, settling_ref, wet, below, species, before, lambda n: send(n).start())
    for n in range(tracers):
        send(n).wait()
    send_t.wait()


def whole(count):
    return [pl.BlockSpec(memory_space=pltpu.VMEM)] * count


def in_hbm(x):
    return pltpu.with_memory_space_constraint(x, pltpu.HBM)


ANY = pl.BlockSpec(memory_space=pl.ANY)
SMEM = pl.BlockSpec(memory_space=pltpu.SMEM)


def params(mib):
    return pltpu.CompilerParams(vmem_limit_bytes=mib * MIB)


def cost(flops, moved):
    return pl.CostEstimate(flops=flops, bytes_accessed=moved, transcendentals=0)


def halo(left_edge, right_edge):
    count = lax.axis_size(AXES)
    ahead = [(i, (i + 1) % count) for i in range(count)]
    return lax.ppermute(right_edge, AXES, ahead), lax.ppermute(left_edge, AXES, [(b, a) for a, b in ahead])


def exchange(pay):
    return lax.all_to_all(pay, AXES, split_axis=0, concat_axis=0, tiled=True)


def body(u, v, temp, salt, species, wet_layers, order, coupling, settling):
    levels, lons, lats = temp.shape
    tracers, _, ctile = species.shape
    tiles = lax.axis_size(AXES)
    cpair = ctile // tiles
    rows = levels * cpair // 128
    field = jax.ShapeDtypeStruct((levels, lons, lats), F32)
    edge = jax.ShapeDtypeStruct((4, levels, lats), F32)
    column = jax.ShapeDtypeStruct((levels, ctile), F32)
    patch = pltpu.HBM((tracers, levels, ctile), F32)
    fcor = (0.8 * jnp.sin(jnp.pi * (jnp.arange(lats, dtype=F32) + 0.5) / lats - jnp.pi / 2))[None]
    sem = pltpu.SemaphoreType.DMA
    mix_flops = 6 * 256 * levels * tracers * ctile
    patch_scratch = pltpu.VMEM((tracers, levels, ctile), F32)
    column_scratch = pltpu.VMEM((levels, ctile), F32)
    onehot_scratch = pltpu.VMEM((ctile, ctile), BF16)

    pay, scale1, heat1 = pl.pallas_call(
        lambda *refs: start_kernel(cpair, *refs),
        out_shape=[pltpu.HBM((tiles, 2 * rows + 8, 128), F32), column, column],
        in_specs=[ANY] * 4,
        out_specs=[ANY] + whole(2),
        scratch_shapes=[
            pltpu.VMEM((lons, lats), jnp.int32),
            pltpu.VMEM((lons, lats), jnp.int32),
            pltpu.VMEM((levels, lons, lats), F32),
            column_scratch,
            pltpu.VMEM((tiles, 2 * rows + 8, 128), F32),
            onehot_scratch,
            pltpu.VMEM((2 * levels + 16, ctile), BF16),
            sem((6,)),
        ],
        compiler_params=params(12),
        name="start",
    )(in_hbm(order), in_hbm(wet_layers), in_hbm(temp), in_hbm(species))
    recv_a = exchange(pay)

    stacked = jnp.stack([u, v, temp, salt])
    left, right = halo(stacked[:, :, 0], stacked[:, :, lons - 1])
    groups = levels * tracers // 256
    react1, first, kron = pl.pallas_call(
        react_kernel,
        out_shape=[patch, jax.ShapeDtypeStruct((2, levels, ctile), F32), jax.ShapeDtypeStruct((512, 256), BF16)],
        in_specs=[ANY] + whole(2),
        out_specs=[ANY] + whole(2),
        scratch_shapes=[patch_scratch, patch_scratch, sem((groups,)), sem((groups,))],
        compiler_params=params(16),
        cost_estimate=cost(mix_flops, 8 * MIB),
        name="react",
    )(in_hbm(species), scale1, coupling)
    pay, u1, v1, x0, s1 = pl.pallas_call(
        lambda *refs: first_tile_kernel(cpair, *refs),
        out_shape=[pltpu.HBM((tiles, 2 * rows, 128), F32)] + [field] * 4,
        in_specs=whole(9),
        out_specs=[ANY] + whole(4),
        scratch_shapes=[pltpu.VMEM((tiles, rows, 128), F32), onehot_scratch, pltpu.VMEM((2 * levels, ctile), BF16), sem((1,))],
        compiler_params=params(12),
        cost_estimate=cost(4 * levels * ctile * ctile, 2 * MIB),
        name="tile_one",
    )(u, v, temp, salt, left, right, wet_layers, fcor, order)

    pay, warm, depth, scale2 = pl.pallas_call(
        lambda *refs: chloro_kernel(cpair, *refs),
        out_shape=[pltpu.HBM(pay.shape, F32), column, jax.ShapeDtypeStruct((8, ctile), F32), column],
        in_specs=[*whole(1), SMEM, *whole(1), ANY],
        out_specs=[ANY, *whole(3)],
        scratch_shapes=[pltpu.VMEM((tiles, rows, 128), F32), sem((1,))],
        input_output_aliases={3: 0},
        compiler_params=params(8),
        name="chloro",
    )(recv_a, settling, first, in_hbm(pay))
    recv_b = exchange(pay)

    recv_a, _ = lax.optimization_barrier((recv_a, pay))
    back, t1, *edges = pl.pallas_call(
        lambda *refs: heat_kernel(cpair, *refs),
        out_shape=[pltpu.HBM((ctile, ctile), BF16), field, edge, edge],
        in_specs=whole(7),
        out_specs=[ANY] + whole(3),
        scratch_shapes=[onehot_scratch, sem((1,))],
        compiler_params=params(12),
        cost_estimate=cost(4 * levels * ctile * ctile, 4 * MIB),
        name="heat",
    )(recv_a, order, wet_layers, u1, v1, x0, s1)
    left, right = halo(*edges)
    species1, react2 = pl.pallas_call(
        tracer_kernel,
        out_shape=[patch, patch],
        in_specs=[ANY] * 2 + whole(5) + [SMEM],
        out_specs=[ANY] * 2,
        scratch_shapes=[patch_scratch] * 2 + [column_scratch] * 2 + [sem((2 * tracers,)), sem((tracers,)), sem((groups,))],
        compiler_params=params(16),
        cost_estimate=cost(mix_flops, 16 * MIB),
        name="tracer",
    )(in_hbm(species), in_hbm(react1), warm, scale2, heat1, depth, kron, settling)
    u2, v2, t2, s2 = pl.pallas_call(
        second_tile_kernel,
        out_shape=[field] * 4,
        in_specs=whole(8),
        out_specs=whole(4),
        compiler_params=params(8),
        cost_estimate=cost(60 * levels * ctile, 2 * MIB),
        name="tile_two",
    )(u1, v1, t1, s1, left, right, wet_layers, fcor)

    species2, t2 = pl.pallas_call(
        lambda *refs: final_kernel(cpair, *refs),
        out_shape=[patch, pltpu.HBM(field.shape, F32)],
        in_specs=[ANY] * 3 + whole(1) + [SMEM] + whole(3),
        out_specs=[ANY] * 2,
        scratch_shapes=[
            patch_scratch,
            patch_scratch,
            onehot_scratch,
            pltpu.VMEM(field.shape, F32),
            column_scratch,
            column_scratch,
            column_scratch,
            sem((2 * tracers,)),
            sem((tracers,)),
            sem((2,)),
        ],
        compiler_params=params(20),
        name="final",
    )(in_hbm(species1), in_hbm(react2), in_hbm(back), depth, settling, recv_b, wet_layers, t2)
    return u2, v2, t2, s2, species2


def solution(mesh):
    tile = P(None, ("groups", "cols", "comp"), None)
    patch = P(None, None, ("groups", "cols", "comp"))
    index = P(("groups", "cols", "comp"), None)
    return jax.shard_map(
        body,
        mesh=mesh,
        in_specs=(tile, tile, tile, tile, patch, index, index, P(), P()),
        out_specs=(tile, tile, tile, tile, patch),
        check_vma=False,
    )
```

```python
import jax
import jax.numpy as jnp
from jax import lax
from jax.experimental import pallas as pl
from jax.experimental.pallas import tpu as pltpu
from jax.sharding import PartitionSpec as P

SUBS = 2
AXES = ("cols", "comp")
F32 = jnp.float32
BF16 = jnp.bfloat16
MIB = 1024 * 1024
BLOCK = 1024


def split(x):
    hi = x.astype(BF16)
    return hi, (x - hi.astype(F32)).astype(BF16)


def split3(x):
    hi = x.astype(BF16)
    rest = x - hi.astype(F32)
    mid = rest.astype(BF16)
    return hi, mid, (rest - mid.astype(F32)).astype(BF16)


def mxu(a, b):
    return jnp.dot(a, b, preferred_element_type=F32)


def iota(shape, dim):
    return lax.broadcasted_iota(jnp.int32, shape, dim)


def pack(out_ref, row, x, cpair):
    groups = 128 // cpair
    rows = x.shape[0] // groups
    lane_group = iota((rows, 128), 1) // cpair
    for e in range(x.shape[1] // 128):
        part = x[:, e * 128 : (e + 1) * 128]
        for o in range(groups):
            out = None
            for g in range(groups):
                piece = part[g * rows : (g + 1) * rows]
                shift = (g - o) * cpair % 128
                if shift:
                    piece = pltpu.roll(piece, shift, 1)
                out = piece if out is None else jnp.where(lane_group == g, piece, out)
            out_ref[e * groups + o, row : row + rows, :] = out


def unpack(in_ref, row, rows, cpair, first, blocks):
    groups = 128 // cpair
    lane_group = iota((rows, 128), 1) // cpair
    columns = []
    for e in range(blocks):
        levels = []
        for g in range(groups):
            out = None
            for o in range(groups):
                piece = in_ref[first + e * groups + o, row : row + rows, :]
                shift = (o - g) * cpair % 128
                if shift:
                    piece = pltpu.roll(piece, shift, 1)
                out = piece if out is None else jnp.where(lane_group == o, piece, out)
            levels.append(out)
        columns.append(jnp.concatenate(levels, axis=0))
    return jnp.concatenate(columns, axis=1)


def running_total(x):
    levels = x.shape[0]
    lower = (iota((levels, levels), 1) <= iota((levels, levels), 0)).astype(F32).astype(BF16)
    return mxu(jnp.concatenate([lower] * 3, axis=1), jnp.concatenate(split3(x), axis=0))


def light(chloro):
    levels = chloro.shape[0]
    trans = jnp.exp(-running_total((0.5 + 0.1 * chloro * chloro) * (1.0 / levels)))
    above = jnp.where(iota(trans.shape, 0) == 0, 1.0, pltpu.roll(trans, 1, 0))
    return trans, levels * (above - trans)


def sink(amounts, fraction):
    for _ in range(SUBS):
        flux = fraction * amounts
        amounts = amounts - flux + pltpu.roll(flux, 1, 0)
    return amounts


def split_kron(coupling):
    tracers = coupling.shape[0]
    size = tracers * 8
    tall = (iota((size, tracers), 0) // 8 == iota((size, tracers), 1)).astype(F32).astype(BF16)
    wide = (iota((tracers, size), 1) // 8 == iota((tracers, size), 0)).astype(F32).astype(BF16)
    same = iota((size, size), 0) % 8 == iota((size, size), 1) % 8
    hi, lo = (jnp.where(same, mxu(mxu(tall, term).astype(BF16), wide), 0.0).astype(BF16) for term in split(coupling))
    return jnp.concatenate([jnp.concatenate([hi, hi], axis=1), jnp.concatenate([lo, jnp.zeros_like(lo)], axis=1)], axis=0)


def mix_levels(kron_ref, tracers_ref, scale_ref, out_ref, first, last):
    tracers, _, columns = tracers_ref.shape
    size = 8 * tracers

    def block(i, _):
        at = pl.ds(pl.multiple_of(i * BLOCK, BLOCK), BLOCK)
        for k in range(first, last, 8):
            hi, lo = split(tracers_ref[:, k : k + 8, at].reshape(size, BLOCK))
            both = mxu(kron_ref[...], jnp.concatenate([hi, lo], axis=0))
            mixed = both[:size] + both[size:]
            out_ref[:, k : k + 8, at] = mixed.reshape(tracers, 8, BLOCK) * scale_ref[k : k + 8, at][None]
        return 0

    lax.fori_loop(0, columns // BLOCK, block, 0)


def sink_all(species_ref, warm_ref, react_ref, depth_ref, settling_ref, wet, below, out_ref, before, after):
    tracers, levels, columns = species_ref.shape
    level = iota((levels, columns), 0).astype(F32)
    depth = depth_ref[0:1, :]
    wet[...] = jnp.where(level < depth, 1.0, 0.0)
    below[...] = jnp.where(level + 1.0 < depth, 1.0, 0.0)

    def one(n, _):
        before(n)
        fraction = settling_ref[n]
        for c in range(0, columns, 128):
            at = slice(c, c + 128)
            amounts = species_ref[n, :, at] + warm_ref[:, at] * react_ref[n, :, at]
            out_ref[n, :, at] = sink(amounts, fraction * below[:, at]) * wet[:, at]
        after(n)
        return 0

    lax.fori_loop(0, tracers, one, 0)


def place_columns(order, onehot, cpair):
    lons, lats = order.shape
    target = iota((lats, lons * lats), 1)
    across = buckets(order, cpair).astype(F32).T.astype(jnp.int32)
    for r in range(lons):
        onehot[r * lats : (r + 1) * lats, :] = jnp.where(target == across[:, r : r + 1], 1.0, 0.0).astype(BF16)


def buckets(order, cpair):
    ctile = order.shape[0] * order.shape[1]
    return (order >> (ctile.bit_length() - 1)) * cpair + (order & (cpair - 1))


def start_kernel(cpair, order_hbm, depth_hbm, temp_hbm, species_hbm, pay_hbm, scale_ref, order, depths, temp, chloro, pay, place, lhs, sems):
    levels, lons, lats = temp.shape
    copies = [
        pltpu.make_async_copy(src, dst, sems.at[i])
        for i, (src, dst) in enumerate(((order_hbm, order), (depth_hbm, depths), (species_hbm.at[0], chloro), (temp_hbm, temp)))
    ]
    for copy in copies:
        copy.start()
    rows = levels * cpair // 128
    copies[0].wait()
    place_columns(order[...], place, cpair)
    copies[1].wait()
    depth = depths[...].astype(F32)
    copies[2].wait()
    trans, heat = light(chloro[...])
    scale_ref[...] = 0.2 * trans
    pack(pay, 0, heat, cpair)
    send_heat = pltpu.make_async_copy(pay.at[:, 0:rows], pay_hbm.at[:, 0:rows], sems.at[4])
    send_heat.start()
    copies[3].wait()
    for r in range(lons):
        hi, lo = split(temp[:, r, :])
        at = slice(r * lats, (r + 1) * lats)
        lhs[0:levels, at] = hi
        lhs[levels : 2 * levels, at] = lo
        lhs[2 * levels : 2 * levels + 16, at] = jnp.broadcast_to(depth[r : r + 1], (16, lats)).astype(BF16)
    sent = mxu(lhs[...], place[...])
    pack(pay, rows, sent[0:levels] + sent[levels : 2 * levels], cpair)
    deep = sent[2 * levels : 2 * levels + 8]
    for d in range(pay.shape[0]):
        e, o = divmod(d * cpair, 128)
        part = deep[:, e * 128 : (e + 1) * 128]
        pay[d, 2 * rows : 2 * rows + 8, :] = pltpu.roll(part, 128 - o, 1) if o else part
    send_temp = pltpu.make_async_copy(pay.at[:, rows : 2 * rows + 8], pay_hbm.at[:, rows : 2 * rows + 8], sems.at[5])
    send_temp.start()
    send_heat.wait()
    send_temp.wait()


def react_kernel(species_hbm, scale_ref, coupling_ref, react_hbm, first_ref, kron_ref, species, react, sems, out_sems):
    tracers, levels, columns = species.shape
    span = 256 // tracers
    parts = [slice(k, k + span) for k in range(0, levels, span)]
    copies = [pltpu.make_async_copy(species_hbm.at[:, at], species.at[:, at], sems.at[i]) for i, at in enumerate(parts)]
    sends = [pltpu.make_async_copy(react.at[:, at], react_hbm.at[:, at], out_sems.at[i]) for i, at in enumerate(parts)]
    for copy in copies:
        copy.start()
    kron_ref[...] = split_kron(coupling_ref[...])
    for copy, send, at in zip(copies, sends, parts):
        copy.wait()
        mix_levels(kron_ref, species, scale_ref, react, at.start, at.stop)
        send.start()
    first_ref[0] = species[0]
    first_ref[1] = react[0]
    for send in sends:
        send.wait()


def tile_levels(fields, depth_ref, fcor_ref, outs):
    levels, lons, lats = fields[0].shape
    shape = (lons, lats)
    lon, lat = iota(shape, 0), iota(shape, 1)
    first_lon, last_lon, first_lat, last_lat = lon == 0, lon == lons - 1, lat == 0, lat == lats - 1
    depth = depth_ref[...]
    turn = jnp.broadcast_to(0.2 * fcor_ref[...], shape)

    def neighbours(f):
        return (
            jnp.where(first_lon, 0.0, pltpu.roll(f, 1, 0)),
            jnp.where(last_lon, 0.0, pltpu.roll(f, lons - 1, 0)),
            jnp.where(first_lat, 0.0, pltpu.roll(f, 1, 1)),
            jnp.where(last_lat, 0.0, pltpu.roll(f, lats - 1, 1)),
        )

    def eight(i, load):
        for j in range(8):
            k = i * 8 + j
            u, v, t, s = (f[k] for f in fields)
            load = load + (0.8 * s - 0.2 * t)
            wet = k < depth
            p0, p1, p2, p3 = neighbours(load)
            u0, u1, u2, u3 = neighbours(u)
            v0, v1, v2, v3 = neighbours(v)
            t0, t1, t2, t3 = neighbours(t)
            s0, s1, s2, s3 = neighbours(s)
            half_u, half_v = 0.1 * u, 0.1 * v
            new_u = 0.92 * u + turn * v - 0.01 * (p1 - p0) + 0.02 * ((u0 + u1) + (u2 + u3))
            new_v = 0.92 * v - turn * u - 0.01 * (p3 - p2) + 0.02 * ((v0 + v1) + (v2 + v3))
            new_t = 0.92 * t - half_u * (t1 - t0) - half_v * (t3 - t2) + 0.02 * ((t0 + t1) + (t2 + t3))
            new_s = 0.92 * s - half_u * (s1 - s0) - half_v * (s3 - s2) + 0.02 * ((s0 + s1) + (s2 + s3))
            for out, new in zip(outs, (new_u, new_v, new_t, new_s)):
                out[k] = jnp.where(wet, new, 0.0)
        return load

    lax.fori_loop(0, levels // 8, eight, jnp.zeros(shape, F32))


def tracer_term(halo, own, depth, sign):
    return jnp.where(iota(halo.shape, 0) < depth, (0.02 + sign * 0.1 * own) * halo, 0.0)


def edge_terms(halo_ref, own, depth, sign):
    wet = iota(own.shape, 0) < depth
    load = running_total(0.8 * halo_ref[3] - 0.2 * halo_ref[2])
    return (
        jnp.where(wet, 0.02 * halo_ref[0] + sign * 0.01 * load, 0.0),
        jnp.where(wet, 0.02 * halo_ref[1], 0.0),
        tracer_term(halo_ref[2], own, depth, sign),
        tracer_term(halo_ref[3], own, depth, sign),
    )


def first_tile_kernel(cpair, u_ref, v_ref, t_ref, s_ref, depth_ref, fcor_ref, order_ref, fields_hbm, sent_ref, edge_ref, fields, place, lhs, sem):
    levels, lons, lats = t_ref.shape
    ctile = lons * lats
    tile_levels((u_ref, v_ref, t_ref, s_ref), depth_ref, fcor_ref, [fields.at[n] for n in range(4)])
    save = pltpu.make_async_copy(fields, fields_hbm, sem.at[0])
    save.start()
    place_columns(order_ref[...], place, cpair)
    edge_ref[0:lats, :] = place[0:lats, :]
    edge_ref[lats : 2 * lats, :] = place[ctile - lats : ctile, :]
    for r in range(lons):
        at = slice(r * lats, (r + 1) * lats)
        lhs[0:levels, at], lhs[levels : 2 * levels, at] = split(fields[2, :, r, :])
    sent = mxu(lhs[...], place[...])
    sent_ref[...] = sent[0:levels] + sent[levels : 2 * levels]
    save.wait()


def chloro_kernel(cpair, recv_ref, settling_ref, first_ref, sent_ref, edge_ref, left_ref, right_ref, first_lon_ref, last_lon_ref, wet_ref,
                  pay_hbm, warm_ref, depth_ref, scale_ref, pay, sems):
    levels, columns = warm_ref.shape
    lons, lats = wet_ref.shape
    rows = levels * cpair // 128
    groups = 128 // cpair
    lane_group = iota((8, 128), 1) // cpair
    for e in range(columns // 128):
        out = None
        for o in range(groups):
            piece = recv_ref[e * groups + o, 2 * rows : 2 * rows + 8, :]
            if o:
                piece = pltpu.roll(piece, o * cpair, 1)
            out = piece if out is None else jnp.where(lane_group == o, piece, out)
        depth_ref[:, e * 128 : (e + 1) * 128] = out
    warm = jnp.exp(0.15 * unpack(recv_ref, rows, rows, cpair, 0, columns // 128))
    warm_ref[...] = warm
    level = iota((levels, columns), 0).astype(F32)
    depth = depth_ref[0:1, :]
    amounts = first_ref[0] + warm * first_ref[1]
    amounts = sink(amounts, jnp.where(level + 1.0 < depth, settling_ref[0], 0.0))
    trans, heat = light(jnp.where(level < depth, amounts, 0.0))
    scale_ref[...] = 0.2 * trans
    pack(pay, rows, heat, cpair)
    send_heat = pltpu.make_async_copy(pay.at[:, rows : 2 * rows], pay_hbm.at[:, rows : 2 * rows], sems.at[0])
    send_heat.start()
    terms = [
        split(tracer_term(halo[2], own[0], wet_ref[lon : lon + 1, :], sign))
        for halo, own, lon, sign in ((left_ref, first_lon_ref, 0, 1.0), (right_ref, last_lon_ref, lons - 1, -1.0))
    ]
    extra = mxu(jnp.concatenate([jnp.concatenate(term, axis=0) for term in terms], axis=1), edge_ref[...])
    pack(pay, 0, sent_ref[...] + (extra[:levels] + extra[levels:]), cpair)
    send_x = pltpu.make_async_copy(pay.at[:, 0:rows], pay_hbm.at[:, 0:rows], sems.at[1])
    send_x.start()
    send_heat.wait()
    send_x.wait()


def back_columns(order, onehot, cpair):
    lons, lats = order.shape
    bucket = buckets(order, cpair)
    source = iota((lons * lats, lats), 0)
    for r in range(lons):
        onehot[:, r * lats : (r + 1) * lats] = jnp.where(source == bucket[r : r + 1], 1.0, 0.0).astype(BF16)


def finish_tile(cpair, recv_ref, row, back_ref, depth_ref, left_ref, right_ref, first_lon_ref, last_lon_ref, fields, out):
    _, levels, lons, lats = out.shape
    ctile = lons * lats
    heat = unpack(recv_ref, row, levels * cpair // 128, cpair, 0, ctile // 128)
    placed = mxu(jnp.concatenate(split(heat), axis=0), back_ref[...])
    placed = 0.2 * (placed[:levels] + placed[levels:])
    for n in (0, 1, 3):
        out[n] = fields[n]
    level = iota((levels, lats), 0)
    for r in range(lons):
        part = placed[:, r * lats : (r + 1) * lats]
        out[2, :, r, :] = fields[2, :, r, :] + jnp.where(level < depth_ref[r : r + 1, :], part, 0.0)
    for halo, own, lon, sign in ((left_ref, first_lon_ref, 0, 1.0), (right_ref, last_lon_ref, lons - 1, -1.0)):
        for n, term in enumerate(edge_terms(halo, own[0], depth_ref[lon : lon + 1, :], sign)):
            out[n, :, lon, :] = out[n, :, lon, :] + term


def heat_kernel(cpair, fields_hbm, recv_ref, order_ref, depth_ref, left_ref, right_ref, first_lon_ref, last_lon_ref,
                out_ref, left_edge_ref, right_edge_ref, fields, back, sem):
    fetch = pltpu.make_async_copy(fields_hbm, fields, sem.at[0])
    fetch.start()
    lons = order_ref.shape[0]
    back_columns(order_ref[...], back, cpair)
    fetch.wait()
    finish_tile(cpair, recv_ref, 0, back, depth_ref, left_ref, right_ref, first_lon_ref, last_lon_ref, fields, out_ref)
    for n in range(4):
        left_edge_ref[n] = out_ref[n, :, 0, :]
        right_edge_ref[n] = out_ref[n, :, lons - 1, :]


def tracer_kernel(species_hbm, react_hbm, warm_ref, scale_ref, depth_ref, kron_ref, settling_ref, out_hbm, next_hbm,
                  species, react, heat, wet, below, in_sems, out_sems, next_sems):
    tracers, levels, columns = species.shape
    span = 256 // tracers

    def fetch(n):
        return (
            pltpu.make_async_copy(species_hbm.at[n], species.at[n], in_sems.at[2 * n]),
            pltpu.make_async_copy(react_hbm.at[n], react.at[n], in_sems.at[2 * n + 1]),
        )

    def save(n):
        return pltpu.make_async_copy(species.at[n], out_hbm.at[n], out_sems.at[n])

    for n in range(tracers):
        for copy in fetch(n):
            copy.start()

    def before(n):
        for copy in fetch(n):
            copy.wait()

        @pl.when(n == 0)
        def _():
            heat[...] = light(species[0])[1]

    sink_all(species, warm_ref, react, depth_ref, settling_ref, wet, below, species, before, lambda n: save(n).start())
    below[...] = scale_ref[...] * jnp.exp(0.03 * (wet[...] * heat[...]))
    parts = [slice(k, k + span) for k in range(0, levels, span)]
    sends = [pltpu.make_async_copy(react.at[:, at], next_hbm.at[:, at], next_sems.at[i]) for i, at in enumerate(parts)]
    for send, at in zip(sends, parts):
        mix_levels(kron_ref, species, below, react, at.start, at.stop)
        send.start()
    for n in range(tracers):
        save(n).wait()
    for send in sends:
        send.wait()


def second_tile_kernel(fields, depth_ref, fcor_ref, out):
    tile_levels([fields.at[n] for n in range(4)], depth_ref, fcor_ref, [out.at[n] for n in range(4)])


def final_kernel(cpair, species_hbm, react_hbm, depth_ref, settling_ref, recv_ref, order_ref, wet_ref, left_ref, right_ref, first_lon_ref, last_lon_ref,
                 fields, out_hbm, *rest):
    field_hbms, (species, react, back, tile, warm, wet, below, in_sems, out_sems, sems) = rest[:4], rest[4:]
    tracers, levels, columns = species.shape
    rows = levels * cpair // 128

    def fetch(n):
        return (
            pltpu.make_async_copy(species_hbm.at[n], species.at[n], in_sems.at[2 * n]),
            pltpu.make_async_copy(react_hbm.at[n], react.at[n], in_sems.at[2 * n + 1]),
        )

    def send(n):
        return pltpu.make_async_copy(species.at[n], out_hbm.at[n], out_sems.at[n])

    for n in range(tracers):
        for copy in fetch(n):
            copy.start()

    def before(n):
        for copy in fetch(n):
            copy.wait()

    back_columns(order_ref[...], back, cpair)
    finish_tile(cpair, recv_ref, rows, back, wet_ref, left_ref, right_ref, first_lon_ref, last_lon_ref, fields, tile)
    sends = [pltpu.make_async_copy(tile.at[n], field_hbms[n], sems.at[n]) for n in range(4)]
    for copy in sends:
        copy.start()
    warm[...] = jnp.exp(0.15 * unpack(recv_ref, 0, rows, cpair, 0, columns // 128))
    sink_all(species, warm, react, depth_ref, settling_ref, wet, below, species, before, lambda n: send(n).start())
    for n in range(tracers):
        send(n).wait()
    for copy in sends:
        copy.wait()


def whole(count):
    return [pl.BlockSpec(memory_space=pltpu.VMEM)] * count


def in_hbm(x):
    return pltpu.with_memory_space_constraint(x, pltpu.HBM)


ANY = pl.BlockSpec(memory_space=pl.ANY)
SMEM = pl.BlockSpec(memory_space=pltpu.SMEM)


def params(mib):
    return pltpu.CompilerParams(vmem_limit_bytes=mib * MIB)


def cost(flops, moved):
    return pl.CostEstimate(flops=flops, bytes_accessed=moved, transcendentals=0)


def halo(left_edge, right_edge):
    count = lax.axis_size(AXES)
    ahead = [(i, (i + 1) % count) for i in range(count)]
    return lax.ppermute(right_edge, AXES, ahead), lax.ppermute(left_edge, AXES, [(b, a) for a, b in ahead])


def exchange(pay):
    return lax.all_to_all(pay, AXES, split_axis=0, concat_axis=0, tiled=True)


def body(u, v, temp, salt, species, wet_layers, order, coupling, settling):
    levels, lons, lats = temp.shape
    tracers, _, ctile = species.shape
    tiles = lax.axis_size(AXES)
    cpair = ctile // tiles
    rows = levels * cpair // 128
    edge = jax.ShapeDtypeStruct((4, levels, lats), F32)
    column = jax.ShapeDtypeStruct((levels, ctile), F32)
    patch = pltpu.HBM((tracers, levels, ctile), F32)
    fcor = (0.8 * jnp.sin(jnp.pi * (jnp.arange(lats, dtype=F32) + 0.5) / lats - jnp.pi / 2))[None]
    sem = pltpu.SemaphoreType.DMA
    mix_flops = 6 * 256 * levels * tracers * ctile
    patch_scratch = pltpu.VMEM((tracers, levels, ctile), F32)
    column_scratch = pltpu.VMEM((levels, ctile), F32)
    onehot_scratch = pltpu.VMEM((ctile, ctile), BF16)

    fields_scratch = pltpu.VMEM((4, levels, lons, lats), F32)

    pay, scale1 = pl.pallas_call(
        lambda *refs: start_kernel(cpair, *refs),
        out_shape=[pltpu.HBM((tiles, 2 * rows + 8, 128), F32), column],
        in_specs=[ANY] * 4,
        out_specs=[ANY] + whole(1),
        scratch_shapes=[
            pltpu.VMEM((lons, lats), jnp.int32),
            pltpu.VMEM((lons, lats), jnp.int32),
            pltpu.VMEM((levels, lons, lats), F32),
            column_scratch,
            pltpu.VMEM((tiles, 2 * rows + 8, 128), F32),
            onehot_scratch,
            pltpu.VMEM((2 * levels + 16, ctile), BF16),
            sem((6,)),
        ],
        compiler_params=params(12),
        name="start",
    )(in_hbm(order), in_hbm(wet_layers), in_hbm(temp), in_hbm(species))
    recv_a = exchange(pay)

    stacked = jnp.stack([u, v, temp, salt])
    edges = stacked[:, :, 0], stacked[:, :, lons - 1]
    left, right = halo(*edges)
    groups = levels * tracers // 256
    react1, first, kron = pl.pallas_call(
        react_kernel,
        out_shape=[patch, jax.ShapeDtypeStruct((2, levels, ctile), F32), jax.ShapeDtypeStruct((16 * tracers, 16 * tracers), BF16)],
        in_specs=[ANY] + whole(2),
        out_specs=[ANY] + whole(2),
        scratch_shapes=[patch_scratch, patch_scratch, sem((groups,)), sem((groups,))],
        compiler_params=params(16),
        cost_estimate=cost(mix_flops, 8 * MIB),
        name="react",
    )(in_hbm(species), scale1, coupling)
    fields1, sent, edge_place = pl.pallas_call(
        lambda *refs: first_tile_kernel(cpair, *refs),
        out_shape=[pltpu.HBM((4, levels, lons, lats), F32), column, jax.ShapeDtypeStruct((2 * lats, ctile), BF16)],
        in_specs=whole(7),
        out_specs=[ANY] + whole(2),
        scratch_shapes=[fields_scratch, onehot_scratch, pltpu.VMEM((2 * levels, ctile), BF16), sem((1,))],
        compiler_params=params(12),
        cost_estimate=cost(4 * levels * ctile * ctile, 2 * MIB),
        name="tile_one",
    )(u, v, temp, salt, wet_layers, fcor, order)

    pay, warm, depth, scale2 = pl.pallas_call(
        lambda *refs: chloro_kernel(cpair, *refs),
        out_shape=[pltpu.HBM((tiles, 2 * rows, 128), F32), column, jax.ShapeDtypeStruct((8, ctile), F32), column],
        in_specs=[*whole(1), SMEM, *whole(8)],
        out_specs=[ANY, *whole(3)],
        scratch_shapes=[pltpu.VMEM((tiles, 2 * rows, 128), F32), sem((2,))],
        compiler_params=params(8),
        name="chloro",
    )(recv_a, settling, first, sent, edge_place, left, right, *edges, wet_layers)
    recv_b = exchange(pay)

    recv_a, _ = lax.optimization_barrier((recv_a, pay))
    fields1, *edges = pl.pallas_call(
        lambda *refs: heat_kernel(cpair, *refs),
        out_shape=[jax.ShapeDtypeStruct((4, levels, lons, lats), F32), edge, edge],
        in_specs=[ANY] + whole(7),
        out_specs=whole(3),
        scratch_shapes=[fields_scratch, onehot_scratch, sem((1,))],
        compiler_params=params(12),
        cost_estimate=cost(4 * levels * ctile * ctile, 4 * MIB),
        name="heat",
    )(in_hbm(fields1), recv_a, order, wet_layers, left, right, *edges)
    left, right = halo(*edges)
    species1, react2 = pl.pallas_call(
        tracer_kernel,
        out_shape=[patch, patch],
        in_specs=[ANY] * 2 + whole(4) + [SMEM],
        out_specs=[ANY] * 2,
        scratch_shapes=[patch_scratch] * 2 + [column_scratch] * 3 + [sem((2 * tracers,)), sem((tracers,)), sem((groups,))],
        compiler_params=params(16),
        cost_estimate=cost(mix_flops, 16 * MIB),
        name="tracer",
    )(in_hbm(species), in_hbm(react1), warm, scale2, depth, kron, settling)
    fields2 = pl.pallas_call(
        second_tile_kernel,
        out_shape=jax.ShapeDtypeStruct((4, levels, lons, lats), F32),
        in_specs=whole(3),
        out_specs=whole(1)[0],
        compiler_params=params(8),
        cost_estimate=cost(60 * levels * ctile, 2 * MIB),
        name="tile_two",
    )(fields1, wet_layers, fcor)

    species2, u2, v2, t2, s2 = pl.pallas_call(
        lambda *refs: final_kernel(cpair, *refs),
        out_shape=[patch] + [pltpu.HBM((levels, lons, lats), F32)] * 4,
        in_specs=[ANY] * 2 + whole(1) + [SMEM] + whole(8),
        out_specs=[ANY] * 5,
        scratch_shapes=[
            patch_scratch,
            patch_scratch,
            onehot_scratch,
            fields_scratch,
            column_scratch,
            column_scratch,
            column_scratch,
            sem((2 * tracers,)),
            sem((tracers,)),
            sem((4,)),
        ],
        compiler_params=params(20),
        name="final",
    )(in_hbm(species1), in_hbm(react2), depth, settling, recv_b, order, wet_layers, left, right, *edges, fields2)
    return u2, v2, t2, s2, species2


def solution(mesh):
    tile = P(None, ("groups", "cols", "comp"), None)
    patch = P(None, None, ("groups", "cols", "comp"))
    index = P(("groups", "cols", "comp"), None)
    return jax.shard_map(
        body,
        mesh=mesh,
        in_specs=(tile, tile, tile, tile, patch, index, index, P(), P()),
        out_specs=(tile, tile, tile, tile, patch),
        check_vma=False,
    )
```

```python
import jax
import jax.numpy as jnp
from jax import lax
from jax.experimental import pallas as pl
from jax.experimental.pallas import tpu as pltpu
from jax.sharding import PartitionSpec as P

SUBS = 2
AXES = ("cols", "comp")
F32 = jnp.float32
BF16 = jnp.bfloat16
MIB = 1024 * 1024
GROUP = 32


def split(x):
    hi = x.astype(BF16)
    return hi, (x - hi.astype(F32)).astype(BF16)


def split3(x):
    hi = x.astype(BF16)
    rest = x - hi.astype(F32)
    mid = rest.astype(BF16)
    return hi, mid, (rest - mid.astype(F32)).astype(BF16)


def mxu(a, b):
    return jnp.dot(a, b, preferred_element_type=F32)


def iota(shape, dim):
    return lax.broadcasted_iota(jnp.int32, shape, dim)


def pack(out_ref, row, x, cpair):
    groups = 128 // cpair
    rows = x.shape[0] // groups
    lane_group = iota((rows, 128), 1) // cpair
    for e in range(x.shape[1] // 128):
        part = x[:, e * 128 : (e + 1) * 128]
        for o in range(groups):
            out = None
            for g in range(groups):
                piece = part[g * rows : (g + 1) * rows]
                shift = (g - o) * cpair % 128
                if shift:
                    piece = pltpu.roll(piece, shift, 1)
                out = piece if out is None else jnp.where(lane_group == g, piece, out)
            out_ref[e * groups + o, row : row + rows, :] = out


def unpack(in_ref, row, rows, cpair, first, blocks):
    groups = 128 // cpair
    lane_group = iota((rows, 128), 1) // cpair
    columns = []
    for e in range(blocks):
        levels = []
        for g in range(groups):
            out = None
            for o in range(groups):
                piece = in_ref[first + e * groups + o, row : row + rows, :]
                shift = (o - g) * cpair % 128
                if shift:
                    piece = pltpu.roll(piece, shift, 1)
                out = piece if out is None else jnp.where(lane_group == o, piece, out)
            levels.append(out)
        columns.append(jnp.concatenate(levels, axis=0))
    return jnp.concatenate(columns, axis=1)


def running_total(x):
    levels = x.shape[0]
    lower = (iota((levels, levels), 1) <= iota((levels, levels), 0)).astype(F32).astype(BF16)
    return mxu(jnp.concatenate([lower] * 3, axis=1), jnp.concatenate(split3(x), axis=0))


def light(chloro):
    levels = chloro.shape[0]
    trans = jnp.exp(-running_total((0.5 + 0.1 * chloro * chloro) * (1.0 / levels)))
    above = jnp.where(iota(trans.shape, 0) == 0, 1.0, pltpu.roll(trans, 1, 0))
    return trans, levels * (above - trans)


def sink(amounts, fraction):
    for _ in range(SUBS):
        flux = fraction * amounts
        amounts = amounts - flux + pltpu.roll(flux, 1, 0)
    return amounts


def split_kron(coupling):
    tracers = coupling.shape[0]
    size = tracers * 8
    tall = (iota((size, tracers), 0) // 8 == iota((size, tracers), 1)).astype(F32).astype(BF16)
    wide = (iota((tracers, size), 1) // 8 == iota((tracers, size), 0)).astype(F32).astype(BF16)
    same = iota((size, size), 0) % 8 == iota((size, size), 1) % 8
    hi, lo = (jnp.where(same, mxu(mxu(tall, term).astype(BF16), wide), 0.0).astype(BF16) for term in split(coupling))
    return jnp.concatenate([jnp.concatenate([hi, hi], axis=1), jnp.concatenate([lo, jnp.zeros_like(lo)], axis=1)], axis=0)


def mix(kron_ref, tracers_ref, out_ref, at):
    tracers, _, columns = tracers_ref.shape
    size = 8 * tracers
    for k in range(at.start, at.stop, 8):
        hi, lo = split(tracers_ref[:, k : k + 8, :].reshape(size, columns))
        both = mxu(kron_ref[...], jnp.concatenate([hi, lo], axis=0))
        out_ref[:, k : k + 8, :] = (both[:size] + both[size:]).reshape(tracers, 8, columns)


def react_and_sink(species, mixed, growth, below, wet, rates_ref, after):
    tracers, _, columns = species.shape

    def one(n, _):
        fraction = rates_ref[n, 0:1, :]
        for c in range(0, columns, 128):
            col = slice(c, c + 128)
            amounts = sink(species[n, :, col] + growth[:, col] * mixed[n, :, col], fraction * below[:, col])
            species[n, :, col] = amounts if wet is None else amounts * wet[:, col]
        return 0

    for i, (first, last) in enumerate(groups(tracers)):
        lax.fori_loop(first, last, one, 0)
        after(i)


def groups(tracers):
    cuts = [0, tracers * 3 // 8, tracers * 11 // 16, tracers * 7 // 8, tracers]
    return list(zip(cuts[:-1], cuts[1:]))


def place_columns(order, onehot, cpair):
    lons, lats = order.shape
    across = buckets(order, cpair).astype(F32).T.astype(jnp.int32)
    lane = iota((lats, 128), 1)
    one, zero = jnp.ones((lats, 128), BF16), jnp.zeros((lats, 128), BF16)
    for r in range(lons):
        own = (jnp.broadcast_to(across[:, r : r + 1], (lats, 128)) - lane).astype(jnp.int16)
        for e in range(0, lons * lats, 128):
            onehot[r * lats : (r + 1) * lats, e : e + 128] = jnp.where(own == jnp.int16(e), one, zero)


def buckets(order, cpair):
    ctile = order.shape[0] * order.shape[1]
    return (order >> (ctile.bit_length() - 1)) * cpair + (order & (cpair - 1))


def start_kernel(cpair, order_hbm, depth_hbm, temp_hbm, species_hbm, pay_hbm, scale_ref, order, depths, temp, chloro, pay, place, lhs, sems):
    levels, lons, lats = temp.shape
    copies = [
        pltpu.make_async_copy(src, dst, sems.at[i])
        for i, (src, dst) in enumerate(((order_hbm, order), (depth_hbm, depths), (species_hbm.at[0], chloro), (temp_hbm, temp)))
    ]
    for copy in copies:
        copy.start()
    rows = levels * cpair // 128
    copies[0].wait()
    place_columns(order[...], place, cpair)
    copies[1].wait()
    depth = depths[...].astype(F32)
    copies[2].wait()
    trans, heat = light(chloro[...])
    scale_ref[...] = 0.2 * trans
    pack(pay, 0, heat, cpair)
    send_heat = pltpu.make_async_copy(pay.at[:, 0:rows], pay_hbm.at[:, 0:rows], sems.at[4])
    send_heat.start()
    copies[3].wait()
    for r in range(lons):
        hi, lo = split(temp[:, r, :])
        at = slice(r * lats, (r + 1) * lats)
        lhs[0:levels, at] = hi
        lhs[levels : 2 * levels, at] = lo
        lhs[2 * levels : 2 * levels + 16, at] = jnp.broadcast_to(depth[r : r + 1], (16, lats)).astype(BF16)
    sent = mxu(lhs[...], place[...])
    pack(pay, rows, sent[0:levels] + sent[levels : 2 * levels], cpair)
    deep = sent[2 * levels : 2 * levels + 8]
    for d in range(pay.shape[0]):
        e, o = divmod(d * cpair, 128)
        part = deep[:, e * 128 : (e + 1) * 128]
        pay[d, 2 * rows : 2 * rows + 8, :] = pltpu.roll(part, 128 - o, 1) if o else part
    send_temp = pltpu.make_async_copy(pay.at[:, rows : 2 * rows + 8], pay_hbm.at[:, rows : 2 * rows + 8], sems.at[5])
    send_temp.start()
    send_heat.wait()
    send_temp.wait()


def react_kernel(species_hbm, scale_ref, coupling_ref, first_ref, species, sems):
    tracers, levels, columns = species.shape
    copies = [pltpu.make_async_copy(species_hbm.at[n], species.at[n], sems.at[n]) for n in range(tracers)]
    for copy in copies:
        copy.start()
    for n, copy in enumerate(copies):
        copy.wait()
        for c in range(0, columns, 128):
            col = slice(c, c + 128)
            term = coupling_ref[0, n] * species[n, :, col]
            first_ref[1, :, col] = first_ref[1, :, col] + term if n else term
    first_ref[0] = species[0]
    first_ref[1] = scale_ref[...] * first_ref[1]


def tile_levels(fields, depth_ref, fcor_ref, outs):
    levels, lons, lats = fields[0].shape
    shape = (lons, lats)
    lon, lat = iota(shape, 0), iota(shape, 1)
    first_lon, last_lon, first_lat, last_lat = lon == 0, lon == lons - 1, lat == 0, lat == lats - 1
    depth = depth_ref[...]
    turn = jnp.broadcast_to(0.2 * fcor_ref[...], shape)

    def neighbours(f):
        return (
            jnp.where(first_lon, 0.0, pltpu.roll(f, 1, 0)),
            jnp.where(last_lon, 0.0, pltpu.roll(f, lons - 1, 0)),
            jnp.where(first_lat, 0.0, pltpu.roll(f, 1, 1)),
            jnp.where(last_lat, 0.0, pltpu.roll(f, lats - 1, 1)),
        )

    def eight(i, load):
        for j in range(8):
            k = i * 8 + j
            u, v, t, s = (f[k] for f in fields)
            load = load + (0.8 * s - 0.2 * t)
            wet = k < depth
            p0, p1, p2, p3 = neighbours(load)
            u0, u1, u2, u3 = neighbours(u)
            v0, v1, v2, v3 = neighbours(v)
            t0, t1, t2, t3 = neighbours(t)
            s0, s1, s2, s3 = neighbours(s)
            half_u, half_v = 0.1 * u, 0.1 * v
            new_u = 0.92 * u + turn * v - 0.01 * (p1 - p0) + 0.02 * ((u0 + u1) + (u2 + u3))
            new_v = 0.92 * v - turn * u - 0.01 * (p3 - p2) + 0.02 * ((v0 + v1) + (v2 + v3))
            new_t = 0.92 * t - half_u * (t1 - t0) - half_v * (t3 - t2) + 0.02 * ((t0 + t1) + (t2 + t3))
            new_s = 0.92 * s - half_u * (s1 - s0) - half_v * (s3 - s2) + 0.02 * ((s0 + s1) + (s2 + s3))
            for out, new in zip(outs, (new_u, new_v, new_t, new_s)):
                out[k] = jnp.where(wet, new, 0.0)
        return load

    lax.fori_loop(0, levels // 8, eight, jnp.zeros(shape, F32))


def tracer_term(halo, own, depth, sign):
    return jnp.where(iota(halo.shape, 0) < depth, (0.02 + sign * 0.1 * own) * halo, 0.0)


def edge_terms(halo_ref, own, depth, sign):
    wet = iota(own.shape, 0) < depth
    load = running_total(0.8 * halo_ref[3] - 0.2 * halo_ref[2])
    return (
        jnp.where(wet, 0.02 * halo_ref[0] + sign * 0.01 * load, 0.0),
        jnp.where(wet, 0.02 * halo_ref[1], 0.0),
        tracer_term(halo_ref[2], own, depth, sign),
        tracer_term(halo_ref[3], own, depth, sign),
    )


def first_tile_kernel(cpair, u_ref, v_ref, t_ref, s_ref, depth_ref, fcor_ref, order_ref, fields_hbm, sent_ref, edge_ref, fields, place, lhs, sem):
    levels, lons, lats = t_ref.shape
    ctile = lons * lats
    tile_levels((u_ref, v_ref, t_ref, s_ref), depth_ref, fcor_ref, [fields.at[n] for n in range(4)])
    save = pltpu.make_async_copy(fields, fields_hbm, sem.at[0])
    save.start()
    place_columns(order_ref[...], place, cpair)
    edge_ref[0:lats, :] = place[0:lats, :]
    edge_ref[lats : 2 * lats, :] = place[ctile - lats : ctile, :]
    for r in range(lons):
        at = slice(r * lats, (r + 1) * lats)
        lhs[0:levels, at], lhs[levels : 2 * levels, at] = split(fields[2, :, r, :])
    sent = mxu(lhs[...], place[...])
    sent_ref[...] = sent[0:levels] + sent[levels : 2 * levels]
    save.wait()


def chloro_kernel(cpair, recv_ref, rates_ref, first_ref, sent_ref, edge_ref, left_ref, right_ref, first_lon_ref, last_lon_ref, wet_ref,
                  pay_hbm, light_hbm, depth_ref, pay, light_ref, sems):
    _, levels, columns = light_ref.shape
    lons, lats = wet_ref.shape
    rows = levels * cpair // 128
    groups = 128 // cpair
    lane_group = iota((8, 128), 1) // cpair
    for e in range(columns // 128):
        out = None
        for o in range(groups):
            piece = recv_ref[e * groups + o, 2 * rows : 2 * rows + 8, :]
            if o:
                piece = pltpu.roll(piece, o * cpair, 1)
            out = piece if out is None else jnp.where(lane_group == o, piece, out)
        depth_ref[:, e * 128 : (e + 1) * 128] = out
    warm = jnp.exp(0.15 * unpack(recv_ref, rows, rows, cpair, 0, columns // 128))
    light_ref[0] = warm
    level = iota((levels, columns), 0).astype(F32)
    depth = depth_ref[0:1, :]
    amounts = first_ref[0] + warm * first_ref[1]
    amounts = sink(amounts, jnp.where(level + 1.0 < depth, rates_ref[0, 0:1, 0:1], 0.0))
    trans, heat = light(jnp.where(level < depth, amounts, 0.0))
    light_ref[1] = 0.2 * trans
    pack(pay, rows, heat, cpair)
    send_heat = pltpu.make_async_copy(pay.at[:, rows : 2 * rows], pay_hbm.at[:, rows : 2 * rows], sems.at[0])
    send_heat.start()
    terms = [
        split(tracer_term(halo[2], own[0], wet_ref[lon : lon + 1, :], sign))
        for halo, own, lon, sign in ((left_ref, first_lon_ref, 0, 1.0), (right_ref, last_lon_ref, lons - 1, -1.0))
    ]
    extra = mxu(jnp.concatenate([jnp.concatenate(term, axis=0) for term in terms], axis=1), edge_ref[...])
    pack(pay, 0, sent_ref[...] + (extra[:levels] + extra[levels:]), cpair)
    send_x = pltpu.make_async_copy(pay.at[:, 0:rows], pay_hbm.at[:, 0:rows], sems.at[1])
    send_x.start()
    save = pltpu.make_async_copy(light_ref, light_hbm, sems.at[2])
    save.start()
    send_heat.wait()
    send_x.wait()
    save.wait()


def back_columns(order, onehot, cpair):
    lons, lats = order.shape
    bucket = buckets(order, cpair)
    row = iota((16, lats), 0)
    one, zero = jnp.ones((16, lats), BF16), jnp.zeros((16, lats), BF16)
    for r in range(lons):
        own = (jnp.broadcast_to(bucket[r : r + 1], (16, lats)) - row).astype(jnp.int16)
        for b in range(0, lons * lats, 16):
            onehot[b : b + 16, r * lats : (r + 1) * lats] = jnp.where(own == jnp.int16(b), one, zero)


def place_heat(cpair, recv_ref, row, back_ref, depth_ref, levels):
    lons, lats = depth_ref.shape
    heat = unpack(recv_ref, row, levels * cpair // 128, cpair, 0, lons * lats // 128)
    placed = mxu(jnp.concatenate(split(heat), axis=0), back_ref[...])
    placed = 0.2 * (placed[:levels] + placed[levels:])
    level = iota((levels, lats), 0)
    return [jnp.where(level < depth_ref[r : r + 1, :], placed[:, r * lats : (r + 1) * lats], 0.0) for r in range(lons)]


def add_edges(depth_ref, left_ref, right_ref, first_lon_ref, last_lon_ref, out):
    lons = depth_ref.shape[0]
    for halo, own, lon, sign in ((left_ref, first_lon_ref, 0, 1.0), (right_ref, last_lon_ref, lons - 1, -1.0)):
        for n, term in enumerate(edge_terms(halo, own[0], depth_ref[lon : lon + 1, :], sign)):
            out[n, :, lon, :] = out[n, :, lon, :] + term


def heat_kernel(cpair, fields_hbm, recv_ref, order_ref, depth_ref, left_ref, right_ref, first_lon_ref, last_lon_ref,
                out_ref, left_edge_ref, right_edge_ref, back, sems):
    lons, lats = order_ref.shape
    fetch = pltpu.make_async_copy(fields_hbm, out_ref, sems.at[0])
    fetch.start()
    back_columns(order_ref[...], back, cpair)
    parts = place_heat(cpair, recv_ref, 0, back, depth_ref, out_ref.shape[1])
    fetch.wait()
    add_edges(depth_ref, left_ref, right_ref, first_lon_ref, last_lon_ref, out_ref)
    for r in range(lons):
        out_ref[2, :, r, :] = out_ref[2, :, r, :] + parts[r]
    for n in range(4):
        left_edge_ref[n] = out_ref[n, :, 0, :]
        right_edge_ref[n] = out_ref[n, :, lons - 1, :]


def tracer_copies(species_hbm, species, out_hbm, in_sems, out_sems):
    ats = [slice(k, k + GROUP) for k in range(0, species.shape[1], GROUP)]
    copies = [pltpu.make_async_copy(species_hbm.at[:, at], species.at[:, at], in_sems.at[i]) for i, at in enumerate(ats)]
    parts = [slice(first, last) for first, last in groups(species.shape[0])]
    sends = [pltpu.make_async_copy(species.at[part], out_hbm.at[part], out_sems.at[i]) for i, part in enumerate(parts)]
    return ats, copies, sends


def tracer_kernel(species_hbm, light_hbm, depth_ref, coupling_ref, rates_ref, fields_ref, wet_ref, fcor_ref,
                  out_hbm, growth_ref, kron_ref, next_fields_ref, species, mixed, light_ref, below, wet, in_sems, out_sems):
    tracers, levels, columns = species.shape
    ats, copies, sends = tracer_copies(species_hbm, species, out_hbm, in_sems, out_sems)
    fetch_light = pltpu.make_async_copy(light_hbm, light_ref, in_sems.at[len(ats)])
    fetch_light.start()
    for copy in copies:
        copy.start()
    kron_ref[...] = split_kron(coupling_ref[...])
    level = iota((levels, columns), 0).astype(F32)
    depth = depth_ref[0:1, :]
    below[...] = jnp.where(level + 1.0 < depth, 1.0, 0.0)
    wet[...] = jnp.where(level < depth, 1.0, 0.0)
    tile_levels([fields_ref.at[n] for n in range(4)], wet_ref, fcor_ref, [next_fields_ref.at[n] for n in range(4)])
    fetch_light.wait()
    for copy, at in zip(copies, ats):
        copy.wait()
        mix(kron_ref, species, mixed, at)
    trans, heat = light(species[0])
    light_ref[0] = 0.2 * trans * light_ref[0]
    growth_ref[...] = wet[...] * (light_ref[1] * jnp.exp(0.03 * (wet[...] * heat)))
    react_and_sink(species, mixed, light_ref.at[0], below, wet, rates_ref, lambda i: sends[i].start())
    for send in sends:
        send.wait()


def final_kernel(cpair, species_hbm, growth_ref, depth_ref, kron_ref, rates_ref, recv_ref, order_ref, wet_ref, left_ref, right_ref,
                 first_lon_ref, last_lon_ref, fields, out_hbm, *rest):
    field_hbms, (species, mixed, back, tile, growth, below, in_sems, out_sems, sems) = rest[:4], rest[4:]
    tracers, levels, columns = species.shape
    rows = levels * cpair // 128
    ats, copies, sends = tracer_copies(species_hbm, species, out_hbm, in_sems, out_sems)
    for copy in copies:
        copy.start()
    tile[...] = fields[...]
    add_edges(wet_ref, left_ref, right_ref, first_lon_ref, last_lon_ref, tile)
    field_sends = [pltpu.make_async_copy(tile.at[n], field_hbms[n], sems.at[n]) for n in range(4)]
    below[...] = jnp.where(iota((levels, columns), 0).astype(F32) + 1.0 < depth_ref[0:1, :], 1.0, 0.0)
    growth[...] = growth_ref[...] * jnp.exp(0.15 * unpack(recv_ref, 0, rows, cpair, 0, columns // 128))
    back_columns(order_ref[...], back, cpair)
    for r, part in enumerate(place_heat(cpair, recv_ref, rows, back, wet_ref, levels)):
        tile[2, :, r, :] = tile[2, :, r, :] + part
    for copy, at in zip(copies, ats):
        copy.wait()
        mix(kron_ref, species, mixed, at)
    for copy in field_sends:
        copy.start()
    react_and_sink(species, mixed, growth, below, None, rates_ref, lambda i: sends[i].start())
    for copy in sends + field_sends:
        copy.wait()


def whole(count):
    return [pl.BlockSpec(memory_space=pltpu.VMEM)] * count


def in_hbm(x):
    return pltpu.with_memory_space_constraint(x, pltpu.HBM)


ANY = pl.BlockSpec(memory_space=pl.ANY)
SMEM = pl.BlockSpec(memory_space=pltpu.SMEM)


def params(mib):
    return pltpu.CompilerParams(vmem_limit_bytes=mib * MIB)


def cost(flops, moved):
    return pl.CostEstimate(flops=flops, bytes_accessed=moved, transcendentals=0)


def halo(left_edge, right_edge):
    count = lax.axis_size(AXES)
    ahead = [(i, (i + 1) % count) for i in range(count)]
    return lax.ppermute(right_edge, AXES, ahead), lax.ppermute(left_edge, AXES, [(b, a) for a, b in ahead])


def exchange(pay):
    return lax.all_to_all(pay, AXES, split_axis=0, concat_axis=0, tiled=True)


def body(u, v, temp, salt, species, wet_layers, order, coupling, settling):
    levels, lons, lats = temp.shape
    tracers, _, ctile = species.shape
    tiles = lax.axis_size(AXES)
    cpair = ctile // tiles
    rows = levels * cpair // 128
    edge = jax.ShapeDtypeStruct((4, levels, lats), F32)
    column = jax.ShapeDtypeStruct((levels, ctile), F32)
    patch = pltpu.HBM((tracers, levels, ctile), F32)
    fcor = (0.8 * jnp.sin(jnp.pi * (jnp.arange(lats, dtype=F32) + 0.5) / lats - jnp.pi / 2))[None]
    rates = jnp.broadcast_to(settling[:, None, None], (tracers, 8, 128))
    sem = pltpu.SemaphoreType.DMA
    mix_flops = 6 * 256 * levels * tracers * ctile
    patch_scratch = pltpu.VMEM((tracers, levels, ctile), F32)
    column_scratch = pltpu.VMEM((levels, ctile), F32)
    onehot_scratch = pltpu.VMEM((ctile, ctile), BF16)

    fields_scratch = pltpu.VMEM((4, levels, lons, lats), F32)

    pay, scale1 = pl.pallas_call(
        lambda *refs: start_kernel(cpair, *refs),
        out_shape=[pltpu.HBM((tiles, 2 * rows + 8, 128), F32), column],
        in_specs=[ANY] * 4,
        out_specs=[ANY] + whole(1),
        scratch_shapes=[
            pltpu.VMEM((lons, lats), jnp.int32),
            pltpu.VMEM((lons, lats), jnp.int32),
            pltpu.VMEM((levels, lons, lats), F32),
            column_scratch,
            pltpu.VMEM((tiles, 2 * rows + 8, 128), F32),
            onehot_scratch,
            pltpu.VMEM((2 * levels + 16, ctile), BF16),
            sem((6,)),
        ],
        compiler_params=params(12),
        name="start",
    )(in_hbm(order), in_hbm(wet_layers), in_hbm(temp), in_hbm(species))
    recv_a = exchange(pay)

    stacked = jnp.stack([u, v, temp, salt])
    edges = stacked[:, :, 0], stacked[:, :, lons - 1]
    left, right = halo(*edges)
    first = pl.pallas_call(
        react_kernel,
        out_shape=jax.ShapeDtypeStruct((2, levels, ctile), F32),
        in_specs=[ANY] + whole(1) + [SMEM],
        out_specs=whole(1)[0],
        scratch_shapes=[patch_scratch, sem((tracers,))],
        compiler_params=params(12),
        cost_estimate=cost(2 * levels * tracers * ctile, 4 * MIB),
        name="react",
    )(in_hbm(species), scale1, coupling)
    fields1, sent, edge_place = pl.pallas_call(
        lambda *refs: first_tile_kernel(cpair, *refs),
        out_shape=[pltpu.HBM((4, levels, lons, lats), F32), column, jax.ShapeDtypeStruct((2 * lats, ctile), BF16)],
        in_specs=whole(7),
        out_specs=[ANY] + whole(2),
        scratch_shapes=[fields_scratch, onehot_scratch, pltpu.VMEM((2 * levels, ctile), BF16), sem((1,))],
        compiler_params=params(12),
        cost_estimate=cost(4 * levels * ctile * ctile, 2 * MIB),
        name="tile_one",
    )(u, v, temp, salt, wet_layers, fcor, order)

    pay, light2, depth = pl.pallas_call(
        lambda *refs: chloro_kernel(cpair, *refs),
        out_shape=[pltpu.HBM((tiles, 2 * rows, 128), F32), pltpu.HBM((2, levels, ctile), F32), jax.ShapeDtypeStruct((8, ctile), F32)],
        in_specs=whole(10),
        out_specs=[ANY, ANY, *whole(1)],
        scratch_shapes=[pltpu.VMEM((tiles, 2 * rows, 128), F32), pltpu.VMEM((2, levels, ctile), F32), sem((3,))],
        compiler_params=params(8),
        name="chloro",
    )(recv_a, rates, first, sent, edge_place, left, right, *edges, wet_layers)
    recv_b = exchange(pay)

    recv_a, _ = lax.optimization_barrier((recv_a, pay))
    fields1, *edges = pl.pallas_call(
        lambda *refs: heat_kernel(cpair, *refs),
        out_shape=[jax.ShapeDtypeStruct((4, levels, lons, lats), F32), edge, edge],
        in_specs=[ANY] + whole(7),
        out_specs=whole(3),
        scratch_shapes=[onehot_scratch, sem((1,))],
        compiler_params=params(12),
        cost_estimate=cost(4 * levels * ctile * ctile, 4 * MIB),
        name="heat",
    )(in_hbm(fields1), recv_a, order, wet_layers, left, right, *edges)
    left, right = halo(*edges)
    steps = levels // GROUP
    species1, growth, kron, fields2 = pl.pallas_call(
        tracer_kernel,
        out_shape=[
            patch,
            column,
            jax.ShapeDtypeStruct((16 * tracers, 16 * tracers), BF16),
            jax.ShapeDtypeStruct((4, levels, lons, lats), F32),
        ],
        in_specs=[ANY] * 2 + whole(6),
        out_specs=[ANY] + whole(3),
        scratch_shapes=[
            patch_scratch,
            patch_scratch,
            pltpu.VMEM((2, levels, ctile), F32),
            column_scratch,
            column_scratch,
            sem((steps + 1,)),
            sem((len(groups(tracers)),)),
        ],
        compiler_params=params(16),
        cost_estimate=cost(mix_flops, 8 * MIB),
        name="tracer",
    )(in_hbm(species), in_hbm(light2), depth, coupling, rates, fields1, wet_layers, fcor)

    species2, u2, v2, t2, s2 = pl.pallas_call(
        lambda *refs: final_kernel(cpair, *refs),
        out_shape=[patch] + [pltpu.HBM((levels, lons, lats), F32)] * 4,
        in_specs=[ANY] + whole(12),
        out_specs=[ANY] * 5,
        scratch_shapes=[
            patch_scratch,
            patch_scratch,
            onehot_scratch,
            fields_scratch,
            column_scratch,
            column_scratch,
            sem((steps,)),
            sem((len(groups(tracers)),)),
            sem((4,)),
        ],
        compiler_params=params(20),
        name="final",
    )(in_hbm(species1), growth, depth, kron, rates, recv_b, order, wet_layers, left, right, *edges, fields2)
    return u2, v2, t2, s2, species2


def solution(mesh):
    tile = P(None, ("groups", "cols", "comp"), None)
    patch = P(None, None, ("groups", "cols", "comp"))
    index = P(("groups", "cols", "comp"), None)
    return jax.shard_map(
        body,
        mesh=mesh,
        in_specs=(tile, tile, tile, tile, patch, index, index, P(), P()),
        out_specs=(tile, tile, tile, tile, patch),
        check_vma=False,
    )
```

```python
import jax
import jax.numpy as jnp
from jax import lax
from jax.experimental import pallas as pl
from jax.experimental.pallas import tpu as pltpu
from jax.sharding import PartitionSpec as P

SUBS = 2
AXES = ("cols", "comp")
F32 = jnp.float32
BF16 = jnp.bfloat16
MIB = 1024 * 1024
FIELDS_AFTER = 1
GROUP = 32


def split(x):
    hi = x.astype(BF16)
    return hi, (x - hi.astype(F32)).astype(BF16)


def split3(x):
    hi = x.astype(BF16)
    rest = x - hi.astype(F32)
    mid = rest.astype(BF16)
    return hi, mid, (rest - mid.astype(F32)).astype(BF16)


def mxu(a, b):
    return jnp.dot(a, b, preferred_element_type=F32)


def iota(shape, dim):
    return lax.broadcasted_iota(jnp.int32, shape, dim)


def pack(out_ref, row, x, cpair):
    groups = 128 // cpair
    rows = x.shape[0] // groups
    lane_group = iota((rows, 128), 1) // cpair
    for e in range(x.shape[1] // 128):
        part = x[:, e * 128 : (e + 1) * 128]
        for o in range(groups):
            out = None
            for g in range(groups):
                piece = part[g * rows : (g + 1) * rows]
                shift = (g - o) * cpair % 128
                if shift:
                    piece = pltpu.roll(piece, shift, 1)
                out = piece if out is None else jnp.where(lane_group == g, piece, out)
            out_ref[e * groups + o, row : row + rows, :] = out


def unpack(in_ref, row, rows, cpair, first, blocks):
    groups = 128 // cpair
    lane_group = iota((rows, 128), 1) // cpair
    columns = []
    for e in range(blocks):
        levels = []
        for g in range(groups):
            out = None
            for o in range(groups):
                piece = in_ref[first + e * groups + o, row : row + rows, :]
                shift = (o - g) * cpair % 128
                if shift:
                    piece = pltpu.roll(piece, shift, 1)
                out = piece if out is None else jnp.where(lane_group == o, piece, out)
            levels.append(out)
        columns.append(jnp.concatenate(levels, axis=0))
    return jnp.concatenate(columns, axis=1)


def running_total(x):
    levels = x.shape[0]
    lower = (iota((levels, levels), 1) <= iota((levels, levels), 0)).astype(F32).astype(BF16)
    return mxu(jnp.concatenate([lower] * 3, axis=1), jnp.concatenate(split3(x), axis=0))


def light(chloro):
    levels = chloro.shape[0]
    trans = jnp.exp(-running_total((0.5 + 0.1 * chloro * chloro) * (1.0 / levels)))
    above = jnp.where(iota(trans.shape, 0) == 0, 1.0, pltpu.roll(trans, 1, 0))
    return trans, levels * (above - trans)


def sink(amounts, fraction):
    for _ in range(SUBS):
        flux = fraction * amounts
        amounts = amounts - flux + pltpu.roll(flux, 1, 0)
    return amounts


def split_kron(coupling):
    tracers = coupling.shape[0]
    size = tracers * 8
    tall = (iota((size, tracers), 0) // 8 == iota((size, tracers), 1)).astype(F32).astype(BF16)
    wide = (iota((tracers, size), 1) // 8 == iota((tracers, size), 0)).astype(F32).astype(BF16)
    same = iota((size, size), 0) % 8 == iota((size, size), 1) % 8
    hi, lo = (jnp.where(same, mxu(mxu(tall, term).astype(BF16), wide), 0.0).astype(BF16) for term in split(coupling))
    return jnp.concatenate([jnp.concatenate([hi, hi], axis=1), jnp.concatenate([lo, jnp.zeros_like(lo)], axis=1)], axis=0)


def mix(kron_ref, tracers_ref, out_ref, at):
    tracers, _, columns = tracers_ref.shape
    size = 8 * tracers
    for k in range(at.start, at.stop, 8):
        hi, lo = split(tracers_ref[:, k : k + 8, :].reshape(size, columns))
        both = mxu(kron_ref[...], jnp.concatenate([hi, lo], axis=0))
        out_ref[:, k : k + 8, :] = (both[:size] + both[size:]).reshape(tracers, 8, columns)


def react_and_sink(species, mixed, growth, below, wet, rates_ref, before, after):
    tracers, _, columns = species.shape

    def one(n, _):
        fraction = rates_ref[n, 0:1, :]
        for c in range(0, columns, 128):
            col = slice(c, c + 128)
            amounts = sink(species[n, :, col] + growth[:, col] * mixed[n, :, col], fraction * below[:, col])
            species[n, :, col] = amounts if wet is None else amounts * wet[:, col]
        return 0

    for i, (first, last) in enumerate(groups(tracers)):
        before(i)
        lax.fori_loop(first, last, one, 0)
        after(i)


def groups(tracers):
    cuts = [tracers * n // 16 for n in (0, 4, 7, 10, 12, 14, 16)]
    return list(zip(cuts[:-1], cuts[1:]))


def place_columns(order, onehot, cpair):
    lons, lats = order.shape
    across = buckets(order, cpair).astype(F32).T.astype(jnp.int32)
    lane = iota((lats, 128), 1)
    one, zero = jnp.ones((lats, 128), BF16), jnp.zeros((lats, 128), BF16)
    for r in range(lons):
        own = (jnp.broadcast_to(across[:, r : r + 1], (lats, 128)) - lane).astype(jnp.int16)
        for e in range(0, lons * lats, 128):
            onehot[r * lats : (r + 1) * lats, e : e + 128] = jnp.where(own == jnp.int16(e), one, zero)


def buckets(order, cpair):
    ctile = order.shape[0] * order.shape[1]
    return (order >> (ctile.bit_length() - 1)) * cpair + (order & (cpair - 1))


def start_kernel(cpair, order_hbm, depth_hbm, temp_hbm, species_hbm, pay_hbm, scale_ref, order, depths, temp, chloro, pay, place, lhs, sems):
    levels, lons, lats = temp.shape
    copies = [
        pltpu.make_async_copy(src, dst, sems.at[i])
        for i, (src, dst) in enumerate(((order_hbm, order), (depth_hbm, depths), (species_hbm.at[0], chloro), (temp_hbm, temp)))
    ]
    for copy in copies:
        copy.start()
    rows = levels * cpair // 128
    copies[0].wait()
    place_columns(order[...], place, cpair)
    copies[1].wait()
    depth = depths[...].astype(F32)
    copies[2].wait()
    trans, heat = light(chloro[...])
    scale_ref[...] = 0.2 * trans
    pack(pay, 0, heat, cpair)
    send_heat = pltpu.make_async_copy(pay.at[:, 0:rows], pay_hbm.at[:, 0:rows], sems.at[4])
    send_heat.start()
    copies[3].wait()
    for r in range(lons):
        hi, lo = split(temp[:, r, :])
        at = slice(r * lats, (r + 1) * lats)
        lhs[0:levels, at] = hi
        lhs[levels : 2 * levels, at] = lo
        lhs[2 * levels : 2 * levels + 16, at] = jnp.broadcast_to(depth[r : r + 1], (16, lats)).astype(BF16)
    sent = mxu(lhs[...], place[...])
    pack(pay, rows, sent[0:levels] + sent[levels : 2 * levels], cpair)
    deep = sent[2 * levels : 2 * levels + 8]
    for d in range(pay.shape[0]):
        e, o = divmod(d * cpair, 128)
        part = deep[:, e * 128 : (e + 1) * 128]
        pay[d, 2 * rows : 2 * rows + 8, :] = pltpu.roll(part, 128 - o, 1) if o else part
    send_temp = pltpu.make_async_copy(pay.at[:, rows : 2 * rows + 8], pay_hbm.at[:, rows : 2 * rows + 8], sems.at[5])
    send_temp.start()
    send_heat.wait()
    send_temp.wait()


def react_kernel(species_hbm, scale_ref, coupling_ref, first_ref, species, sems):
    tracers, levels, columns = species.shape
    copies = [pltpu.make_async_copy(species_hbm.at[n], species.at[n], sems.at[n]) for n in range(tracers)]
    for copy in copies:
        copy.start()
    for n, copy in enumerate(copies):
        copy.wait()
        for c in range(0, columns, 128):
            col = slice(c, c + 128)
            term = coupling_ref[0, n] * species[n, :, col]
            first_ref[1, :, col] = first_ref[1, :, col] + term if n else term
    first_ref[0] = species[0]
    first_ref[1] = scale_ref[...] * first_ref[1]


def tile_levels(fields, depth_ref, fcor_ref, outs):
    levels, lons, lats = fields[0].shape
    shape = (lons, lats)
    lon, lat = iota(shape, 0), iota(shape, 1)
    first_lon, last_lon, first_lat, last_lat = lon == 0, lon == lons - 1, lat == 0, lat == lats - 1
    depth = depth_ref[...]
    turn = jnp.broadcast_to(0.2 * fcor_ref[...], shape)

    def neighbours(f):
        return (
            jnp.where(first_lon, 0.0, pltpu.roll(f, 1, 0)),
            jnp.where(last_lon, 0.0, pltpu.roll(f, lons - 1, 0)),
            jnp.where(first_lat, 0.0, pltpu.roll(f, 1, 1)),
            jnp.where(last_lat, 0.0, pltpu.roll(f, lats - 1, 1)),
        )

    def eight(i, load):
        for j in range(8):
            k = i * 8 + j
            u, v, t, s = (f[k] for f in fields)
            load = load + (0.8 * s - 0.2 * t)
            wet = k < depth
            p0, p1, p2, p3 = neighbours(load)
            u0, u1, u2, u3 = neighbours(u)
            v0, v1, v2, v3 = neighbours(v)
            t0, t1, t2, t3 = neighbours(t)
            s0, s1, s2, s3 = neighbours(s)
            half_u, half_v = 0.1 * u, 0.1 * v
            new_u = 0.92 * u + turn * v - 0.01 * (p1 - p0) + 0.02 * ((u0 + u1) + (u2 + u3))
            new_v = 0.92 * v - turn * u - 0.01 * (p3 - p2) + 0.02 * ((v0 + v1) + (v2 + v3))
            new_t = 0.92 * t - half_u * (t1 - t0) - half_v * (t3 - t2) + 0.02 * ((t0 + t1) + (t2 + t3))
            new_s = 0.92 * s - half_u * (s1 - s0) - half_v * (s3 - s2) + 0.02 * ((s0 + s1) + (s2 + s3))
            for out, new in zip(outs, (new_u, new_v, new_t, new_s)):
                out[k] = jnp.where(wet, new, 0.0)
        return load

    lax.fori_loop(0, levels // 8, eight, jnp.zeros(shape, F32))


def tracer_term(halo, own, depth, sign):
    return jnp.where(iota(halo.shape, 0) < depth, (0.02 + sign * 0.1 * own) * halo, 0.0)


def edge_terms(halo_ref, own, depth, sign):
    wet = iota(own.shape, 0) < depth
    load = running_total(0.8 * halo_ref[3] - 0.2 * halo_ref[2])
    return (
        jnp.where(wet, 0.02 * halo_ref[0] + sign * 0.01 * load, 0.0),
        jnp.where(wet, 0.02 * halo_ref[1], 0.0),
        tracer_term(halo_ref[2], own, depth, sign),
        tracer_term(halo_ref[3], own, depth, sign),
    )


def first_tile_kernel(cpair, u_ref, v_ref, t_ref, s_ref, depth_ref, fcor_ref, order_ref, fields_hbm, sent_ref, edge_ref, fields, place, lhs, sem):
    levels, lons, lats = t_ref.shape
    ctile = lons * lats
    tile_levels((u_ref, v_ref, t_ref, s_ref), depth_ref, fcor_ref, [fields.at[n] for n in range(4)])
    save = pltpu.make_async_copy(fields, fields_hbm, sem.at[0])
    save.start()
    place_columns(order_ref[...], place, cpair)
    edge_ref[0:lats, :] = place[0:lats, :]
    edge_ref[lats : 2 * lats, :] = place[ctile - lats : ctile, :]
    for r in range(lons):
        at = slice(r * lats, (r + 1) * lats)
        lhs[0:levels, at], lhs[levels : 2 * levels, at] = split(fields[2, :, r, :])
    sent = mxu(lhs[...], place[...])
    sent_ref[...] = sent[0:levels] + sent[levels : 2 * levels]
    save.wait()


def chloro_kernel(cpair, recv_ref, rates_ref, first_ref, sent_ref, edge_ref, left_ref, right_ref, first_lon_ref, last_lon_ref, wet_ref,
                  pay_hbm, light_hbm, depth_ref, pay, light_ref, sems):
    _, levels, columns = light_ref.shape
    lons, lats = wet_ref.shape
    rows = levels * cpair // 128
    groups = 128 // cpair
    lane_group = iota((8, 128), 1) // cpair
    for e in range(columns // 128):
        out = None
        for o in range(groups):
            piece = recv_ref[e * groups + o, 2 * rows : 2 * rows + 8, :]
            if o:
                piece = pltpu.roll(piece, o * cpair, 1)
            out = piece if out is None else jnp.where(lane_group == o, piece, out)
        depth_ref[:, e * 128 : (e + 1) * 128] = out
    warm = jnp.exp(0.15 * unpack(recv_ref, rows, rows, cpair, 0, columns // 128))
    light_ref[0] = warm
    level = iota((levels, columns), 0).astype(F32)
    depth = depth_ref[0:1, :]
    amounts = first_ref[0] + warm * first_ref[1]
    amounts = sink(amounts, jnp.where(level + 1.0 < depth, rates_ref[0, 0:1, 0:1], 0.0))
    trans, heat = light(jnp.where(level < depth, amounts, 0.0))
    light_ref[1] = 0.2 * trans
    pack(pay, rows, heat, cpair)
    send_heat = pltpu.make_async_copy(pay.at[:, rows : 2 * rows], pay_hbm.at[:, rows : 2 * rows], sems.at[0])
    send_heat.start()
    terms = [
        split(tracer_term(halo[2], own[0], wet_ref[lon : lon + 1, :], sign))
        for halo, own, lon, sign in ((left_ref, first_lon_ref, 0, 1.0), (right_ref, last_lon_ref, lons - 1, -1.0))
    ]
    extra = mxu(jnp.concatenate([jnp.concatenate(term, axis=0) for term in terms], axis=1), edge_ref[...])
    pack(pay, 0, sent_ref[...] + (extra[:levels] + extra[levels:]), cpair)
    send_x = pltpu.make_async_copy(pay.at[:, 0:rows], pay_hbm.at[:, 0:rows], sems.at[1])
    send_x.start()
    save = pltpu.make_async_copy(light_ref, light_hbm, sems.at[2])
    save.start()
    send_heat.wait()
    send_x.wait()
    save.wait()


def back_columns(order, onehot, cpair):
    lons, lats = order.shape
    bucket = buckets(order, cpair)
    row = iota((16, lats), 0)
    one, zero = jnp.ones((16, lats), BF16), jnp.zeros((16, lats), BF16)
    for r in range(lons):
        own = (jnp.broadcast_to(bucket[r : r + 1], (16, lats)) - row).astype(jnp.int16)
        for b in range(0, lons * lats, 16):
            onehot[b : b + 16, r * lats : (r + 1) * lats] = jnp.where(own == jnp.int16(b), one, zero)


def place_heat(cpair, recv_ref, row, back_ref, depth_ref, levels):
    lons, lats = depth_ref.shape
    heat = unpack(recv_ref, row, levels * cpair // 128, cpair, 0, lons * lats // 128)
    placed = mxu(jnp.concatenate(split(heat), axis=0), back_ref[...])
    placed = 0.2 * (placed[:levels] + placed[levels:])
    level = iota((levels, lats), 0)
    return [jnp.where(level < depth_ref[r : r + 1, :], placed[:, r * lats : (r + 1) * lats], 0.0) for r in range(lons)]


def add_edges(depth_ref, left_ref, right_ref, first_lon_ref, last_lon_ref, out):
    lons = depth_ref.shape[0]
    for halo, own, lon, sign in ((left_ref, first_lon_ref, 0, 1.0), (right_ref, last_lon_ref, lons - 1, -1.0)):
        for n, term in enumerate(edge_terms(halo, own[0], depth_ref[lon : lon + 1, :], sign)):
            out[n, :, lon, :] = out[n, :, lon, :] + term


def heat_kernel(cpair, fields_hbm, recv_ref, order_ref, depth_ref, left_ref, right_ref, first_lon_ref, last_lon_ref,
                out_ref, left_edge_ref, right_edge_ref, back, sems):
    lons, lats = order_ref.shape
    fetch = pltpu.make_async_copy(fields_hbm, out_ref, sems.at[0])
    fetch.start()
    back_columns(order_ref[...], back, cpair)
    parts = place_heat(cpair, recv_ref, 0, back, depth_ref, out_ref.shape[1])
    fetch.wait()
    add_edges(depth_ref, left_ref, right_ref, first_lon_ref, last_lon_ref, out_ref)
    for r in range(lons):
        out_ref[2, :, r, :] = out_ref[2, :, r, :] + parts[r]
    for n in range(4):
        left_edge_ref[n] = out_ref[n, :, 0, :]
        right_edge_ref[n] = out_ref[n, :, lons - 1, :]


def group_copies(src, dst, sems):
    parts = [slice(first, last) for first, last in groups(src.shape[0])]
    return [pltpu.make_async_copy(src.at[part], dst.at[part], sems.at[i]) for i, part in enumerate(parts)]


def level_copies(src, dst, sems):
    ats = [slice(k, k + GROUP) for k in range(0, src.shape[1], GROUP)]
    return ats, [pltpu.make_async_copy(src.at[:, at], dst.at[:, at], sems.at[i]) for i, at in enumerate(ats)]


def tracer_kernel(species_hbm, light_hbm, depth_ref, coupling_ref, rates_ref, fields_ref, wet_ref, fcor_ref,
                  out_hbm, mixed_hbm, growth_ref, next_fields_ref, species, mixed, kron_ref, light_ref, below, wet, in_sems, out_sems, mixed_sems):
    tracers, levels, columns = species.shape
    ats, copies = level_copies(species_hbm, species, in_sems)
    sends = group_copies(species, out_hbm, out_sems)
    _, mixed_sends = level_copies(mixed, mixed_hbm, mixed_sems)
    fetch_light = pltpu.make_async_copy(light_hbm, light_ref, in_sems.at[len(ats)])
    fetch_light.start()
    for copy in copies:
        copy.start()
    kron_ref[...] = split_kron(coupling_ref[...])
    level = iota((levels, columns), 0).astype(F32)
    depth = depth_ref[0:1, :]
    below[...] = jnp.where(level + 1.0 < depth, 1.0, 0.0)
    wet[...] = jnp.where(level < depth, 1.0, 0.0)
    tile_levels([fields_ref.at[n] for n in range(4)], wet_ref, fcor_ref, [next_fields_ref.at[n] for n in range(4)])
    fetch_light.wait()
    for copy, at in zip(copies, ats):
        copy.wait()
        mix(kron_ref, species, mixed, at)
    trans, heat = light(species[0])
    light_ref[0] = 0.2 * trans * light_ref[0]
    growth_ref[...] = wet[...] * (light_ref[1] * jnp.exp(0.03 * (wet[...] * heat)))
    react_and_sink(species, mixed, light_ref.at[0], below, wet, rates_ref, lambda i: None, lambda i: sends[i].start())
    for send, at in zip(mixed_sends, ats):
        mix(kron_ref, species, mixed, at)
        send.start()
    for send in sends + mixed_sends:
        send.wait()


def final_kernel(cpair, species_hbm, mixed_hbm, growth_ref, depth_ref, rates_ref, recv_ref, order_ref, wet_ref, left_ref, right_ref,
                 first_lon_ref, last_lon_ref, fields, out_hbm, *rest):
    field_hbms, (species, mixed, back, tile, growth, below, in_sems, mixed_sems, out_sems, sems) = rest[:4], rest[4:]
    tracers, levels, columns = species.shape
    rows = levels * cpair // 128
    copies = list(zip(group_copies(species_hbm, species, in_sems), group_copies(mixed_hbm, mixed, mixed_sems)))
    sends = group_copies(species, out_hbm, out_sems)
    for pair in copies:
        for copy in pair:
            copy.start()
    tile[...] = fields[...]
    add_edges(wet_ref, left_ref, right_ref, first_lon_ref, last_lon_ref, tile)
    field_sends = [pltpu.make_async_copy(tile.at[n], field_hbms[n], sems.at[n]) for n in range(4)]
    below[...] = jnp.where(iota((levels, columns), 0).astype(F32) + 1.0 < depth_ref[0:1, :], 1.0, 0.0)
    growth[...] = growth_ref[...] * jnp.exp(0.15 * unpack(recv_ref, 0, rows, cpair, 0, columns // 128))
    back_columns(order_ref[...], back, cpair)
    for r, part in enumerate(place_heat(cpair, recv_ref, rows, back, wet_ref, levels)):
        tile[2, :, r, :] = tile[2, :, r, :] + part

    def before(i):
        for copy in copies[i]:
            copy.wait()

    def after(i):
        sends[i].start()
        if i == FIELDS_AFTER:
            for copy in field_sends:
                copy.start()

    react_and_sink(species, mixed, growth, below, None, rates_ref, before, after)
    for copy in sends + field_sends:
        copy.wait()


def whole(count):
    return [pl.BlockSpec(memory_space=pltpu.VMEM)] * count


def in_hbm(x):
    return pltpu.with_memory_space_constraint(x, pltpu.HBM)


ANY = pl.BlockSpec(memory_space=pl.ANY)
SMEM = pl.BlockSpec(memory_space=pltpu.SMEM)


def params(mib):
    return pltpu.CompilerParams(vmem_limit_bytes=mib * MIB)


def cost(flops, moved):
    return pl.CostEstimate(flops=flops, bytes_accessed=moved, transcendentals=0)


def halo(left_edge, right_edge):
    count = lax.axis_size(AXES)
    ahead = [(i, (i + 1) % count) for i in range(count)]
    return lax.ppermute(right_edge, AXES, ahead), lax.ppermute(left_edge, AXES, [(b, a) for a, b in ahead])


def exchange(pay):
    return lax.all_to_all(pay, AXES, split_axis=0, concat_axis=0, tiled=True)


def body(u, v, temp, salt, species, wet_layers, order, coupling, settling):
    levels, lons, lats = temp.shape
    tracers, _, ctile = species.shape
    tiles = lax.axis_size(AXES)
    cpair = ctile // tiles
    rows = levels * cpair // 128
    edge = jax.ShapeDtypeStruct((4, levels, lats), F32)
    column = jax.ShapeDtypeStruct((levels, ctile), F32)
    patch = pltpu.HBM((tracers, levels, ctile), F32)
    fcor = (0.8 * jnp.sin(jnp.pi * (jnp.arange(lats, dtype=F32) + 0.5) / lats - jnp.pi / 2))[None]
    rates = jnp.broadcast_to(settling[:, None, None], (tracers, 8, 128))
    sem = pltpu.SemaphoreType.DMA
    mix_flops = 6 * 256 * levels * tracers * ctile
    patch_scratch = pltpu.VMEM((tracers, levels, ctile), F32)
    column_scratch = pltpu.VMEM((levels, ctile), F32)
    onehot_scratch = pltpu.VMEM((ctile, ctile), BF16)

    fields_scratch = pltpu.VMEM((4, levels, lons, lats), F32)

    pay, scale1 = pl.pallas_call(
        lambda *refs: start_kernel(cpair, *refs),
        out_shape=[pltpu.HBM((tiles, 2 * rows + 8, 128), F32), column],
        in_specs=[ANY] * 4,
        out_specs=[ANY] + whole(1),
        scratch_shapes=[
            pltpu.VMEM((lons, lats), jnp.int32),
            pltpu.VMEM((lons, lats), jnp.int32),
            pltpu.VMEM((levels, lons, lats), F32),
            column_scratch,
            pltpu.VMEM((tiles, 2 * rows + 8, 128), F32),
            onehot_scratch,
            pltpu.VMEM((2 * levels + 16, ctile), BF16),
            sem((6,)),
        ],
        compiler_params=params(12),
        name="start",
    )(in_hbm(order), in_hbm(wet_layers), in_hbm(temp), in_hbm(species))
    recv_a = exchange(pay)

    stacked = jnp.stack([u, v, temp, salt])
    edges = stacked[:, :, 0], stacked[:, :, lons - 1]
    left, right = halo(*edges)
    first = pl.pallas_call(
        react_kernel,
        out_shape=jax.ShapeDtypeStruct((2, levels, ctile), F32),
        in_specs=[ANY] + whole(1) + [SMEM],
        out_specs=whole(1)[0],
        scratch_shapes=[patch_scratch, sem((tracers,))],
        compiler_params=params(12),
        cost_estimate=cost(2 * levels * tracers * ctile, 4 * MIB),
        name="react",
    )(in_hbm(species), scale1, coupling)
    fields1, sent, edge_place = pl.pallas_call(
        lambda *refs: first_tile_kernel(cpair, *refs),
        out_shape=[pltpu.HBM((4, levels, lons, lats), F32), column, jax.ShapeDtypeStruct((2 * lats, ctile), BF16)],
        in_specs=whole(7),
        out_specs=[ANY] + whole(2),
        scratch_shapes=[fields_scratch, onehot_scratch, pltpu.VMEM((2 * levels, ctile), BF16), sem((1,))],
        compiler_params=params(12),
        cost_estimate=cost(4 * levels * ctile * ctile, 2 * MIB),
        name="tile_one",
    )(u, v, temp, salt, wet_layers, fcor, order)

    pay, light2, depth = pl.pallas_call(
        lambda *refs: chloro_kernel(cpair, *refs),
        out_shape=[pltpu.HBM((tiles, 2 * rows, 128), F32), pltpu.HBM((2, levels, ctile), F32), jax.ShapeDtypeStruct((8, ctile), F32)],
        in_specs=whole(10),
        out_specs=[ANY, ANY, *whole(1)],
        scratch_shapes=[pltpu.VMEM((tiles, 2 * rows, 128), F32), pltpu.VMEM((2, levels, ctile), F32), sem((3,))],
        compiler_params=params(8),
        name="chloro",
    )(recv_a, rates, first, sent, edge_place, left, right, *edges, wet_layers)
    recv_b = exchange(pay)

    recv_a, _ = lax.optimization_barrier((recv_a, pay))
    fields1, *edges = pl.pallas_call(
        lambda *refs: heat_kernel(cpair, *refs),
        out_shape=[jax.ShapeDtypeStruct((4, levels, lons, lats), F32), edge, edge],
        in_specs=[ANY] + whole(7),
        out_specs=whole(3),
        scratch_shapes=[onehot_scratch, sem((1,))],
        compiler_params=params(12),
        cost_estimate=cost(4 * levels * ctile * ctile, 4 * MIB),
        name="heat",
    )(in_hbm(fields1), recv_a, order, wet_layers, left, right, *edges)
    left, right = halo(*edges)
    steps = levels // GROUP
    species1, mixed, growth, fields2 = pl.pallas_call(
        tracer_kernel,
        out_shape=[
            patch,
            patch,
            column,
            jax.ShapeDtypeStruct((4, levels, lons, lats), F32),
        ],
        in_specs=[ANY] * 2 + whole(6),
        out_specs=[ANY] * 2 + whole(2),
        scratch_shapes=[
            patch_scratch,
            patch_scratch,
            pltpu.VMEM((16 * tracers, 16 * tracers), BF16),
            pltpu.VMEM((2, levels, ctile), F32),
            column_scratch,
            column_scratch,
            sem((steps + 1,)),
            sem((len(groups(tracers)),)),
            sem((steps,)),
        ],
        compiler_params=params(16),
        cost_estimate=cost(mix_flops, 8 * MIB),
        name="tracer",
    )(in_hbm(species), in_hbm(light2), depth, coupling, rates, fields1, wet_layers, fcor)

    species2, u2, v2, t2, s2 = pl.pallas_call(
        lambda *refs: final_kernel(cpair, *refs),
        out_shape=[patch] + [pltpu.HBM((levels, lons, lats), F32)] * 4,
        in_specs=[ANY] * 2 + whole(11),
        out_specs=[ANY] * 5,
        scratch_shapes=[
            patch_scratch,
            patch_scratch,
            onehot_scratch,
            fields_scratch,
            column_scratch,
            column_scratch,
            sem((len(groups(tracers)),)),
            sem((len(groups(tracers)),)),
            sem((len(groups(tracers)),)),
            sem((4,)),
        ],
        compiler_params=params(20),
        name="final",
    )(in_hbm(species1), in_hbm(mixed), growth, depth, rates, recv_b, order, wet_layers, left, right, *edges, fields2)
    return u2, v2, t2, s2, species2


def solution(mesh):
    tile = P(None, ("groups", "cols", "comp"), None)
    patch = P(None, None, ("groups", "cols", "comp"))
    index = P(("groups", "cols", "comp"), None)
    return jax.shard_map(
        body,
        mesh=mesh,
        in_specs=(tile, tile, tile, tile, patch, index, index, P(), P()),
        out_specs=(tile, tile, tile, tile, patch),
        check_vma=False,
    )
```

```python
import jax
import jax.numpy as jnp
from jax import lax
from jax.experimental import pallas as pl
from jax.experimental.pallas import tpu as pltpu
from jax.sharding import PartitionSpec as P

SUBS = 2
AXES = ("cols", "comp")
F32 = jnp.float32
BF16 = jnp.bfloat16
MIB = 1024 * 1024
FIELDS_AFTER = 1
UNIT = 2
GROUP = 32


def split(x):
    hi = x.astype(BF16)
    return hi, (x - hi.astype(F32)).astype(BF16)


def split3(x):
    hi = x.astype(BF16)
    rest = x - hi.astype(F32)
    mid = rest.astype(BF16)
    return hi, mid, (rest - mid.astype(F32)).astype(BF16)


def mxu(a, b):
    return jnp.dot(a, b, preferred_element_type=F32)


def iota(shape, dim):
    return lax.broadcasted_iota(jnp.int32, shape, dim)


def put(ref, d, row, x):
    if len(ref.shape) == 3:
        ref[d, row : row + x.shape[0], :] = x
    else:
        for i in range(0, x.shape[0], UNIT):
            ref[d, (row + i) // UNIT] = x[i : i + UNIT]


def get(ref, d, row, rows):
    if len(ref.shape) == 3:
        return ref[d, row : row + rows, :]
    return jnp.concatenate([ref[d, (row + i) // UNIT] for i in range(0, rows, UNIT)], axis=0)


def pack(out_ref, row, x, cpair):
    groups = 128 // cpair
    rows = x.shape[0] // groups
    lane_group = iota((rows, 128), 1) // cpair
    for e in range(x.shape[1] // 128):
        part = x[:, e * 128 : (e + 1) * 128]
        for o in range(groups):
            out = None
            for g in range(groups):
                piece = part[g * rows : (g + 1) * rows]
                shift = (g - o) * cpair % 128
                if shift:
                    piece = pltpu.roll(piece, shift, 1)
                out = piece if out is None else jnp.where(lane_group == g, piece, out)
            put(out_ref, e * groups + o, row, out)


def unpack(in_ref, row, rows, cpair, first, blocks):
    groups = 128 // cpair
    lane_group = iota((rows, 128), 1) // cpair
    columns = []
    for e in range(blocks):
        pieces = [get(in_ref, first + e * groups + o, row, rows) for o in range(groups)]
        levels = []
        for g in range(groups):
            out = None
            for o, piece in enumerate(pieces):
                shift = (o - g) * cpair % 128
                if shift:
                    piece = pltpu.roll(piece, shift, 1)
                out = piece if out is None else jnp.where(lane_group == o, piece, out)
            levels.append(out)
        columns.append(jnp.concatenate(levels, axis=0))
    return jnp.concatenate(columns, axis=1)


def running_total(x):
    levels = x.shape[0]
    lower = (iota((levels, levels), 1) <= iota((levels, levels), 0)).astype(F32).astype(BF16)
    return mxu(jnp.concatenate([lower] * 3, axis=1), jnp.concatenate(split3(x), axis=0))


def light(chloro):
    levels = chloro.shape[0]
    trans = jnp.exp(-running_total((0.5 + 0.1 * chloro * chloro) * (1.0 / levels)))
    above = jnp.where(iota(trans.shape, 0) == 0, 1.0, pltpu.roll(trans, 1, 0))
    return trans, levels * (above - trans)


def sink(amounts, fraction):
    for _ in range(SUBS):
        flux = fraction * amounts
        amounts = amounts - flux + pltpu.roll(flux, 1, 0)
    return amounts


def split_kron(coupling):
    tracers = coupling.shape[0]
    size = tracers * 8
    tall = (iota((size, tracers), 0) // 8 == iota((size, tracers), 1)).astype(F32).astype(BF16)
    wide = (iota((tracers, size), 1) // 8 == iota((tracers, size), 0)).astype(F32).astype(BF16)
    same = iota((size, size), 0) % 8 == iota((size, size), 1) % 8
    hi, lo = (jnp.where(same, mxu(mxu(tall, term).astype(BF16), wide), 0.0).astype(BF16) for term in split(coupling))
    return jnp.concatenate([jnp.concatenate([hi, hi], axis=1), jnp.concatenate([lo, jnp.zeros_like(lo)], axis=1)], axis=0)


def mix(kron_ref, tracers_ref, out_ref, at):
    tracers, _, columns = tracers_ref.shape
    size = 8 * tracers
    for k in range(at.start, at.stop, 8):
        hi, lo = split(tracers_ref[:, k : k + 8, :].reshape(size, columns))
        both = mxu(kron_ref[...], jnp.concatenate([hi, lo], axis=0))
        out_ref[:, k : k + 8, :] = (both[:size] + both[size:]).reshape(tracers, 8, columns)


def react_and_sink(species, mixed, growth, below, wet, rates_ref, before, after):
    tracers, _, columns = species.shape

    def one(n, _):
        fraction = rates_ref[n, 0:1, :]
        for c in range(0, columns, 128):
            col = slice(c, c + 128)
            amounts = sink(species[n, :, col] + growth[:, col] * mixed[n, :, col], fraction * below[:, col])
            species[n, :, col] = amounts if wet is None else amounts * wet[:, col]
        return 0

    for i, (first, last) in enumerate(groups(tracers)):
        before(i)
        lax.fori_loop(first, last, one, 0)
        after(i)


def groups(tracers):
    cuts = [tracers * n // 16 for n in (0, 4, 7, 10, 12, 14, 16)]
    return list(zip(cuts[:-1], cuts[1:]))


def place_columns(order, onehot, cpair):
    lons, lats = order.shape
    across = buckets(order, cpair).astype(F32).T.astype(jnp.int32)
    lane = iota((lats, 128), 1)
    one, zero = jnp.ones((lats, 128), BF16), jnp.zeros((lats, 128), BF16)
    for r in range(lons):
        own = (jnp.broadcast_to(across[:, r : r + 1], (lats, 128)) - lane).astype(jnp.int16)
        for e in range(0, lons * lats, 128):
            onehot[r * lats : (r + 1) * lats, e : e + 128] = jnp.where(own == jnp.int16(e), one, zero)


def buckets(order, cpair):
    ctile = order.shape[0] * order.shape[1]
    return (order >> (ctile.bit_length() - 1)) * cpair + (order & (cpair - 1))


def start_kernel(cpair, order_hbm, depth_hbm, temp_hbm, species_hbm, pay_hbm, scale_ref, order, depths, temp, chloro, pay, place, lhs, sems):
    levels, lons, lats = temp.shape
    copies = [
        pltpu.make_async_copy(src, dst, sems.at[i])
        for i, (src, dst) in enumerate(((order_hbm, order), (depth_hbm, depths), (species_hbm.at[0], chloro), (temp_hbm, temp)))
    ]
    for copy in copies:
        copy.start()
    rows = levels * cpair // 128
    copies[0].wait()
    place_columns(order[...], place, cpair)
    copies[1].wait()
    depth = depths[...].astype(F32)
    copies[2].wait()
    trans, heat = light(chloro[...])
    scale_ref[...] = 0.2 * trans
    pack(pay, 0, heat, cpair)
    send_heat = pltpu.make_async_copy(pay.at[:, 0 : rows // UNIT], pay_hbm.at[:, 0 : rows // UNIT], sems.at[4])
    send_heat.start()
    copies[3].wait()
    for r in range(lons):
        hi, lo = split(temp[:, r, :])
        at = slice(r * lats, (r + 1) * lats)
        lhs[0:levels, at] = hi
        lhs[levels : 2 * levels, at] = lo
        lhs[2 * levels : 2 * levels + 16, at] = jnp.broadcast_to(depth[r : r + 1], (16, lats)).astype(BF16)
    sent = mxu(lhs[...], place[...])
    pack(pay, rows, sent[0:levels] + sent[levels : 2 * levels], cpair)
    deep = sent[2 * levels : 2 * levels + UNIT]
    for d in range(pay.shape[0]):
        e, o = divmod(d * cpair, 128)
        part = deep[:, e * 128 : (e + 1) * 128]
        pay[d, 2 * rows // UNIT] = pltpu.roll(part, 128 - o, 1) if o else part
    send_temp = pltpu.make_async_copy(pay.at[:, rows // UNIT :], pay_hbm.at[:, rows // UNIT :], sems.at[5])
    send_temp.start()
    send_heat.wait()
    send_temp.wait()


def react_kernel(species_hbm, scale_ref, coupling_ref, first_ref, species, sems):
    tracers, levels, columns = species.shape
    copies = [pltpu.make_async_copy(species_hbm.at[n], species.at[n], sems.at[n]) for n in range(tracers)]
    for copy in copies:
        copy.start()
    for n, copy in enumerate(copies):
        copy.wait()
        for c in range(0, columns, 128):
            col = slice(c, c + 128)
            term = coupling_ref[0, n] * species[n, :, col]
            first_ref[1, :, col] = first_ref[1, :, col] + term if n else term
    first_ref[0] = species[0]
    first_ref[1] = scale_ref[...] * first_ref[1]


def tile_levels(fields, depth_ref, fcor_ref, outs):
    levels, lons, lats = fields[0].shape
    shape = (lons, lats)
    lon, lat = iota(shape, 0), iota(shape, 1)
    first_lon, last_lon, first_lat, last_lat = lon == 0, lon == lons - 1, lat == 0, lat == lats - 1
    depth = depth_ref[...]
    turn = jnp.broadcast_to(0.2 * fcor_ref[...], shape)

    def neighbours(f):
        return (
            jnp.where(first_lon, 0.0, pltpu.roll(f, 1, 0)),
            jnp.where(last_lon, 0.0, pltpu.roll(f, lons - 1, 0)),
            jnp.where(first_lat, 0.0, pltpu.roll(f, 1, 1)),
            jnp.where(last_lat, 0.0, pltpu.roll(f, lats - 1, 1)),
        )

    def eight(i, load):
        for j in range(8):
            k = i * 8 + j
            u, v, t, s = (f[k] for f in fields)
            load = load + (0.8 * s - 0.2 * t)
            wet = k < depth
            p0, p1, p2, p3 = neighbours(load)
            u0, u1, u2, u3 = neighbours(u)
            v0, v1, v2, v3 = neighbours(v)
            t0, t1, t2, t3 = neighbours(t)
            s0, s1, s2, s3 = neighbours(s)
            half_u, half_v = 0.1 * u, 0.1 * v
            new_u = 0.92 * u + turn * v - 0.01 * (p1 - p0) + 0.02 * ((u0 + u1) + (u2 + u3))
            new_v = 0.92 * v - turn * u - 0.01 * (p3 - p2) + 0.02 * ((v0 + v1) + (v2 + v3))
            new_t = 0.92 * t - half_u * (t1 - t0) - half_v * (t3 - t2) + 0.02 * ((t0 + t1) + (t2 + t3))
            new_s = 0.92 * s - half_u * (s1 - s0) - half_v * (s3 - s2) + 0.02 * ((s0 + s1) + (s2 + s3))
            for out, new in zip(outs, (new_u, new_v, new_t, new_s)):
                out[k] = jnp.where(wet, new, 0.0)
        return load

    lax.fori_loop(0, levels // 8, eight, jnp.zeros(shape, F32))


def tracer_term(halo, own, depth, sign):
    return jnp.where(iota(halo.shape, 0) < depth, (0.02 + sign * 0.1 * own) * halo, 0.0)


def edge_terms(halo_ref, own, depth, sign):
    wet = iota(own.shape, 0) < depth
    load = running_total(0.8 * halo_ref[3] - 0.2 * halo_ref[2])
    return (
        jnp.where(wet, 0.02 * halo_ref[0] + sign * 0.01 * load, 0.0),
        jnp.where(wet, 0.02 * halo_ref[1], 0.0),
        tracer_term(halo_ref[2], own, depth, sign),
        tracer_term(halo_ref[3], own, depth, sign),
    )


def first_tile_kernel(cpair, u_ref, v_ref, t_ref, s_ref, depth_ref, fcor_ref, order_ref, fields_hbm, sent_ref, edge_ref, fields, place, lhs, sem):
    levels, lons, lats = t_ref.shape
    ctile = lons * lats
    tile_levels((u_ref, v_ref, t_ref, s_ref), depth_ref, fcor_ref, [fields.at[n] for n in range(4)])
    save = pltpu.make_async_copy(fields, fields_hbm, sem.at[0])
    save.start()
    place_columns(order_ref[...], place, cpair)
    edge_ref[0:lats, :] = place[0:lats, :]
    edge_ref[lats : 2 * lats, :] = place[ctile - lats : ctile, :]
    for r in range(lons):
        at = slice(r * lats, (r + 1) * lats)
        lhs[0:levels, at], lhs[levels : 2 * levels, at] = split(fields[2, :, r, :])
    sent = mxu(lhs[...], place[...])
    sent_ref[...] = sent[0:levels] + sent[levels : 2 * levels]
    save.wait()


def chloro_kernel(cpair, recv_ref, rates_ref, first_ref, sent_ref, edge_ref, left_ref, right_ref, first_lon_ref, last_lon_ref, wet_ref,
                  pay_hbm, light_hbm, depth_ref, pay, light_ref, sems):
    _, levels, columns = light_ref.shape
    lons, lats = wet_ref.shape
    rows = levels * cpair // 128
    groups = 128 // cpair
    lane_group = iota((UNIT, 128), 1) // cpair
    for e in range(columns // 128):
        out = None
        for o in range(groups):
            piece = recv_ref[e * groups + o, 2 * rows // UNIT]
            if o:
                piece = pltpu.roll(piece, o * cpair, 1)
            out = piece if out is None else jnp.where(lane_group == o, piece, out)
        depth_ref[0:UNIT, e * 128 : (e + 1) * 128] = out
    warm = jnp.exp(0.15 * unpack(recv_ref, rows, rows, cpair, 0, columns // 128))
    light_ref[0] = warm
    level = iota((levels, columns), 0).astype(F32)
    depth = depth_ref[0:1, :]
    amounts = first_ref[0] + warm * first_ref[1]
    amounts = sink(amounts, jnp.where(level + 1.0 < depth, rates_ref[0, 0:1, 0:1], 0.0))
    trans, heat = light(jnp.where(level < depth, amounts, 0.0))
    light_ref[1] = 0.2 * trans
    pack(pay, rows, heat, cpair)
    send_heat = pltpu.make_async_copy(pay.at[:, rows : 2 * rows], pay_hbm.at[:, rows : 2 * rows], sems.at[0])
    send_heat.start()
    terms = [
        split(tracer_term(halo[2], own[0], wet_ref[lon : lon + 1, :], sign))
        for halo, own, lon, sign in ((left_ref, first_lon_ref, 0, 1.0), (right_ref, last_lon_ref, lons - 1, -1.0))
    ]
    extra = mxu(jnp.concatenate([jnp.concatenate(term, axis=0) for term in terms], axis=1), edge_ref[...])
    pack(pay, 0, sent_ref[...] + (extra[:levels] + extra[levels:]), cpair)
    send_x = pltpu.make_async_copy(pay.at[:, 0:rows], pay_hbm.at[:, 0:rows], sems.at[1])
    send_x.start()
    save = pltpu.make_async_copy(light_ref, light_hbm, sems.at[2])
    save.start()
    send_heat.wait()
    send_x.wait()
    save.wait()


def back_columns(order, onehot, cpair):
    lons, lats = order.shape
    bucket = buckets(order, cpair)
    row = iota((16, lats), 0)
    one, zero = jnp.ones((16, lats), BF16), jnp.zeros((16, lats), BF16)
    for r in range(lons):
        own = (jnp.broadcast_to(bucket[r : r + 1], (16, lats)) - row).astype(jnp.int16)
        for b in range(0, lons * lats, 16):
            onehot[b : b + 16, r * lats : (r + 1) * lats] = jnp.where(own == jnp.int16(b), one, zero)


def place_heat(cpair, recv_ref, row, back_ref, depth_ref, levels):
    lons, lats = depth_ref.shape
    heat = unpack(recv_ref, row, levels * cpair // 128, cpair, 0, lons * lats // 128)
    placed = mxu(jnp.concatenate(split(heat), axis=0), back_ref[...])
    placed = 0.2 * (placed[:levels] + placed[levels:])
    level = iota((levels, lats), 0)
    return [jnp.where(level < depth_ref[r : r + 1, :], placed[:, r * lats : (r + 1) * lats], 0.0) for r in range(lons)]


def add_edges(depth_ref, left_ref, right_ref, first_lon_ref, last_lon_ref, out):
    lons = depth_ref.shape[0]
    for halo, own, lon, sign in ((left_ref, first_lon_ref, 0, 1.0), (right_ref, last_lon_ref, lons - 1, -1.0)):
        for n, term in enumerate(edge_terms(halo, own[0], depth_ref[lon : lon + 1, :], sign)):
            out[n, :, lon, :] = out[n, :, lon, :] + term


def heat_kernel(cpair, fields_hbm, recv_ref, order_ref, depth_ref, left_ref, right_ref, first_lon_ref, last_lon_ref,
                out_ref, left_edge_ref, right_edge_ref, back, sems):
    lons, lats = order_ref.shape
    fetch = pltpu.make_async_copy(fields_hbm, out_ref, sems.at[0])
    fetch.start()
    back_columns(order_ref[...], back, cpair)
    parts = place_heat(cpair, recv_ref, 0, back, depth_ref, out_ref.shape[1])
    fetch.wait()
    add_edges(depth_ref, left_ref, right_ref, first_lon_ref, last_lon_ref, out_ref)
    for r in range(lons):
        out_ref[2, :, r, :] = out_ref[2, :, r, :] + parts[r]
    for n in range(4):
        left_edge_ref[n] = out_ref[n, :, 0, :]
        right_edge_ref[n] = out_ref[n, :, lons - 1, :]


def group_copies(src, dst, sems):
    parts = [slice(first, last) for first, last in groups(src.shape[0])]
    return [pltpu.make_async_copy(src.at[part], dst.at[part], sems.at[i]) for i, part in enumerate(parts)]


def level_copies(src, dst, sems):
    ats = [slice(k, k + GROUP) for k in range(0, src.shape[1], GROUP)]
    return ats, [pltpu.make_async_copy(src.at[:, at], dst.at[:, at], sems.at[i]) for i, at in enumerate(ats)]


def tracer_kernel(species_hbm, light_hbm, depth_ref, coupling_ref, rates_ref, fields_ref, wet_ref, fcor_ref,
                  out_hbm, mixed_hbm, growth_ref, next_fields_ref, species, mixed, kron_ref, light_ref, below, wet, in_sems, out_sems, mixed_sems):
    tracers, levels, columns = species.shape
    ats, copies = level_copies(species_hbm, species, in_sems)
    sends = group_copies(species, out_hbm, out_sems)
    _, mixed_sends = level_copies(mixed, mixed_hbm, mixed_sems)
    fetch_light = pltpu.make_async_copy(light_hbm, light_ref, in_sems.at[len(ats)])
    fetch_light.start()
    for copy in copies:
        copy.start()
    kron_ref[...] = split_kron(coupling_ref[...])
    level = iota((levels, columns), 0).astype(F32)
    depth = depth_ref[0:1, :]
    below[...] = jnp.where(level + 1.0 < depth, 1.0, 0.0)
    wet[...] = jnp.where(level < depth, 1.0, 0.0)
    tile_levels([fields_ref.at[n] for n in range(4)], wet_ref, fcor_ref, [next_fields_ref.at[n] for n in range(4)])
    fetch_light.wait()
    for copy, at in zip(copies, ats):
        copy.wait()
        mix(kron_ref, species, mixed, at)
    trans, heat = light(species[0])
    light_ref[0] = 0.2 * trans * light_ref[0]
    growth_ref[...] = wet[...] * (light_ref[1] * jnp.exp(0.03 * (wet[...] * heat)))
    react_and_sink(species, mixed, light_ref.at[0], below, wet, rates_ref, lambda i: None, lambda i: sends[i].start())
    for send, at in zip(mixed_sends, ats):
        mix(kron_ref, species, mixed, at)
        send.start()
    for send in sends + mixed_sends:
        send.wait()


def final_kernel(cpair, species_hbm, mixed_hbm, growth_ref, depth_ref, rates_ref, recv_ref, order_ref, wet_ref, left_ref, right_ref,
                 first_lon_ref, last_lon_ref, fields, out_hbm, *rest):
    field_hbms, (species, mixed, back, tile, growth, below, in_sems, mixed_sems, out_sems, sems) = rest[:4], rest[4:]
    tracers, levels, columns = species.shape
    rows = levels * cpair // 128
    copies = list(zip(group_copies(species_hbm, species, in_sems), group_copies(mixed_hbm, mixed, mixed_sems)))
    sends = group_copies(species, out_hbm, out_sems)
    for pair in copies:
        for copy in pair:
            copy.start()
    tile[...] = fields[...]
    add_edges(wet_ref, left_ref, right_ref, first_lon_ref, last_lon_ref, tile)
    field_sends = [pltpu.make_async_copy(tile.at[n], field_hbms[n], sems.at[n]) for n in range(4)]
    below[...] = jnp.where(iota((levels, columns), 0).astype(F32) + 1.0 < depth_ref[0:1, :], 1.0, 0.0)
    growth[...] = growth_ref[...] * jnp.exp(0.15 * unpack(recv_ref, 0, rows, cpair, 0, columns // 128))
    back_columns(order_ref[...], back, cpair)
    for r, part in enumerate(place_heat(cpair, recv_ref, rows, back, wet_ref, levels)):
        tile[2, :, r, :] = tile[2, :, r, :] + part

    def before(i):
        for copy in copies[i]:
            copy.wait()

    def after(i):
        sends[i].start()
        if i == FIELDS_AFTER:
            for copy in field_sends:
                copy.start()

    react_and_sink(species, mixed, growth, below, None, rates_ref, before, after)
    for copy in sends + field_sends:
        copy.wait()


def whole(count):
    return [pl.BlockSpec(memory_space=pltpu.VMEM)] * count


def in_hbm(x):
    return pltpu.with_memory_space_constraint(x, pltpu.HBM)


ANY = pl.BlockSpec(memory_space=pl.ANY)
SMEM = pl.BlockSpec(memory_space=pltpu.SMEM)


def params(mib):
    return pltpu.CompilerParams(vmem_limit_bytes=mib * MIB)


def cost(flops, moved):
    return pl.CostEstimate(flops=flops, bytes_accessed=moved, transcendentals=0)


def halo(left_edge, right_edge):
    count = lax.axis_size(AXES)
    ahead = [(i, (i + 1) % count) for i in range(count)]
    return lax.ppermute(right_edge, AXES, ahead), lax.ppermute(left_edge, AXES, [(b, a) for a, b in ahead])


def exchange(pay):
    return lax.all_to_all(pay, AXES, split_axis=0, concat_axis=0, tiled=True)


def body(u, v, temp, salt, species, wet_layers, order, coupling, settling):
    levels, lons, lats = temp.shape
    tracers, _, ctile = species.shape
    tiles = lax.axis_size(AXES)
    cpair = ctile // tiles
    rows = levels * cpair // 128
    edge = jax.ShapeDtypeStruct((4, levels, lats), F32)
    column = jax.ShapeDtypeStruct((levels, ctile), F32)
    patch = pltpu.HBM((tracers, levels, ctile), F32)
    fcor = (0.8 * jnp.sin(jnp.pi * (jnp.arange(lats, dtype=F32) + 0.5) / lats - jnp.pi / 2))[None]
    rates = jnp.broadcast_to(settling[:, None, None], (tracers, 8, 128))
    sem = pltpu.SemaphoreType.DMA
    mix_flops = 6 * 256 * levels * tracers * ctile
    patch_scratch = pltpu.VMEM((tracers, levels, ctile), F32)
    column_scratch = pltpu.VMEM((levels, ctile), F32)
    onehot_scratch = pltpu.VMEM((ctile, ctile), BF16)

    fields_scratch = pltpu.VMEM((4, levels, lons, lats), F32)

    pay, scale1 = pl.pallas_call(
        lambda *refs: start_kernel(cpair, *refs),
        out_shape=[pltpu.HBM((tiles, 2 * rows // UNIT + 1, UNIT, 128), F32), column],
        in_specs=[ANY] * 4,
        out_specs=[ANY] + whole(1),
        scratch_shapes=[
            pltpu.VMEM((lons, lats), jnp.int32),
            pltpu.VMEM((lons, lats), jnp.int32),
            pltpu.VMEM((levels, lons, lats), F32),
            column_scratch,
            pltpu.VMEM((tiles, 2 * rows // UNIT + 1, UNIT, 128), F32),
            onehot_scratch,
            pltpu.VMEM((2 * levels + 16, ctile), BF16),
            sem((6,)),
        ],
        compiler_params=params(12),
        name="start",
    )(in_hbm(order), in_hbm(wet_layers), in_hbm(temp), in_hbm(species))
    recv_a = exchange(pay)

    stacked = jnp.stack([u, v, temp, salt])
    edges = stacked[:, :, 0], stacked[:, :, lons - 1]
    left, right = halo(*edges)
    first = pl.pallas_call(
        react_kernel,
        out_shape=jax.ShapeDtypeStruct((2, levels, ctile), F32),
        in_specs=[ANY] + whole(1) + [SMEM],
        out_specs=whole(1)[0],
        scratch_shapes=[patch_scratch, sem((tracers,))],
        compiler_params=params(12),
        cost_estimate=cost(2 * levels * tracers * ctile, 4 * MIB),
        name="react",
    )(in_hbm(species), scale1, coupling)
    fields1, sent, edge_place = pl.pallas_call(
        lambda *refs: first_tile_kernel(cpair, *refs),
        out_shape=[pltpu.HBM((4, levels, lons, lats), F32), column, jax.ShapeDtypeStruct((2 * lats, ctile), BF16)],
        in_specs=whole(7),
        out_specs=[ANY] + whole(2),
        scratch_shapes=[fields_scratch, onehot_scratch, pltpu.VMEM((2 * levels, ctile), BF16), sem((1,))],
        compiler_params=params(12),
        cost_estimate=cost(4 * levels * ctile * ctile, 2 * MIB),
        name="tile_one",
    )(u, v, temp, salt, wet_layers, fcor, order)

    pay, light2, depth = pl.pallas_call(
        lambda *refs: chloro_kernel(cpair, *refs),
        out_shape=[pltpu.HBM((tiles, 2 * rows, 128), F32), pltpu.HBM((2, levels, ctile), F32), jax.ShapeDtypeStruct((8, ctile), F32)],
        in_specs=whole(10),
        out_specs=[ANY, ANY, *whole(1)],
        scratch_shapes=[pltpu.VMEM((tiles, 2 * rows, 128), F32), pltpu.VMEM((2, levels, ctile), F32), sem((3,))],
        compiler_params=params(8),
        name="chloro",
    )(recv_a, rates, first, sent, edge_place, left, right, *edges, wet_layers)
    recv_b = exchange(pay)

    recv_a, _ = lax.optimization_barrier((recv_a, pay))
    fields1, *edges = pl.pallas_call(
        lambda *refs: heat_kernel(cpair, *refs),
        out_shape=[jax.ShapeDtypeStruct((4, levels, lons, lats), F32), edge, edge],
        in_specs=[ANY] + whole(7),
        out_specs=whole(3),
        scratch_shapes=[onehot_scratch, sem((1,))],
        compiler_params=params(12),
        cost_estimate=cost(4 * levels * ctile * ctile, 4 * MIB),
        name="heat",
    )(in_hbm(fields1), recv_a, order, wet_layers, left, right, *edges)
    left, right = halo(*edges)
    steps = levels // GROUP
    species1, mixed, growth, fields2 = pl.pallas_call(
        tracer_kernel,
        out_shape=[
            patch,
            patch,
            column,
            jax.ShapeDtypeStruct((4, levels, lons, lats), F32),
        ],
        in_specs=[ANY] * 2 + whole(6),
        out_specs=[ANY] * 2 + whole(2),
        scratch_shapes=[
            patch_scratch,
            patch_scratch,
            pltpu.VMEM((16 * tracers, 16 * tracers), BF16),
            pltpu.VMEM((2, levels, ctile), F32),
            column_scratch,
            column_scratch,
            sem((steps + 1,)),
            sem((len(groups(tracers)),)),
            sem((steps,)),
        ],
        compiler_params=params(16),
        cost_estimate=cost(mix_flops, 8 * MIB),
        name="tracer",
    )(in_hbm(species), in_hbm(light2), depth, coupling, rates, fields1, wet_layers, fcor)

    species2, u2, v2, t2, s2 = pl.pallas_call(
        lambda *refs: final_kernel(cpair, *refs),
        out_shape=[patch] + [pltpu.HBM((levels, lons, lats), F32)] * 4,
        in_specs=[ANY] * 2 + whole(11),
        out_specs=[ANY] * 5,
        scratch_shapes=[
            patch_scratch,
            patch_scratch,
            onehot_scratch,
            fields_scratch,
            column_scratch,
            column_scratch,
            sem((len(groups(tracers)),)),
            sem((len(groups(tracers)),)),
            sem((len(groups(tracers)),)),
            sem((4,)),
        ],
        compiler_params=params(20),
        name="final",
    )(in_hbm(species1), in_hbm(mixed), growth, depth, rates, recv_b, order, wet_layers, left, right, *edges, fields2)
    return u2, v2, t2, s2, species2


def solution(mesh):
    tile = P(None, ("groups", "cols", "comp"), None)
    patch = P(None, None, ("groups", "cols", "comp"))
    index = P(("groups", "cols", "comp"), None)
    return jax.shard_map(
        body,
        mesh=mesh,
        in_specs=(tile, tile, tile, tile, patch, index, index, P(), P()),
        out_specs=(tile, tile, tile, tile, patch),
        check_vma=False,
    )
```
